256 devices in a mesh: grp: 16 (over z_hi, x, core), gz: 16 (over z_lo, y).
Axes of the slice: x: 4, y: 4, z: 8 (z_hi: 2, z_lo: 4; z = z_hi * 4 + z_lo), core: 2. Of those that a mesh axis runs over, the one named last changes fastest.
Arguments:
- pet_image: float32 [128, 32, 480], P('gz'), may hold values from 0.5 to 2
- mr_image: float32 [128, 32, 960], P('gz'), may hold values from -6 to 6
- coil_sens: bfloat16 [32, 128, 32, 960], P('grp', 'gz'), may hold values from -0.8984375 to 0.8984375
- kspace_data: bfloat16 [32, 128, 32, 960], P('grp', None, 'gz'), may hold values from -1.1953125 to 1.1953125
- kspace_mask: int32 [128, 480], replicated, may hold values 0 or 1
- system_tiles: bfloat16 [4096, 128, 480], P(('grp', 'gz')), may hold values from 0.0099487305 to 4
- tile_subset_block: int32 [4096], P(('grp', 'gz')), may hold values from 0 to 15
- tile_col: int32 [4096], P(('grp', 'gz')), may hold values from 0 to 255
- measured: float32 [1024, 128], P('grp'), may hold values from 0 to 24
- background: float32 [1024, 128], P('grp'), may hold values from 0.5 to 2
- subset_view_blocks: int32 [256], P('grp'), may hold values from 0 to 63
Outputs:
- grad_pet: float32 [128, 32, 480], P('gz', 'grp')
- grad_mr: float32 [128, 32, 960], P('gz', 'grp')
The draws below stay inside these ranges and needn't reach their ends.
All inputs are finite; a program needn't handle non-finite values.
Results may differ from the reference program's by a relative error of at most 0.0036.
Values may be sent and summed in bfloat16 or wider, within the bound.
No kernel may reach another device: no remote copies, remote signals or barrier semaphores. Data moves between devices by JAX's collectives and lax.ppermute only.
A program may use at most 64 MiB of HBM per device.

```python
import math
import jax
import jax.numpy as jnp
from jax import lax

Y_CELLS = 480
ZS = 8
NXW = 32
BLOCK_BINS = 128
SUBSET_BLOCKS = 16
VIEWSET_BLOCKS = 64
TPD = 16
NZ = 128
COILS = 32
TILES = 4096
N_GRP = 16
N_GZ = 16


def set_ends(entries, rng, least, top_value):
    dims = entries.shape
    place = [jax.random.randint(jax.random.fold_in(rng, axis), (), 0, dims[axis]) for axis in range(len(dims))]
    entries = entries.at[tuple(place)].set(least)
    longest = dims.index(max(dims))
    place[longest] = (place[longest] + 1) % dims[longest]
    return entries.at[tuple(place)].set(top_value)


def spiked(entries, own_key, source, target, parts, factor):
    owner, partner = [(jnp.arange(entries.shape[dim]) // (entries.shape[dim] // parts)).reshape([-1 if axis == dim else 1 for axis in range(entries.ndim)]) for dim in (source, target)]
    chosen = jax.random.permutation(own_key, parts)[partner]
    strong = (owner == chosen) | (owner == (partner + parts // 2) % parts)
    return jnp.where(strong, factor * entries, entries)


def block_levels(stream_key, shape, split, smallest, high):
    def one(dim, shards_of):
        heights = jax.random.uniform(jax.random.fold_in(jax.random.fold_in(stream_key, 6), dim), (shards_of,), jnp.float32, smallest / len(split), high / len(split))
        return jnp.repeat(jnp.exp(heights), shape[dim] // shards_of).reshape((-1,) + (1,) * (len(shape) - dim - 1))

    loudness = one(*split[0])
    for cut in split[1:]:
        loudness = loudness * one(*cut)
    return loudness


def bell_draw(rng, shape, deviation, limit, split=(), held_as=jnp.bfloat16):
    array = jax.random.normal(rng, shape, jnp.float32) * deviation
    if len(split) > 0:
        array = block_levels(rng, shape, split, -0.22, 0.18) * array
    return jnp.clip(array, min=-limit, max=limit).astype(held_as)


def noise_with(stream_key, dims, scale, limit, pieces, heavy, kind=jnp.bfloat16):
    values = scale * jax.random.normal(stream_key, dims, jnp.float32)
    if pieces:
        values = values * block_levels(stream_key, dims, pieces, -0.22, 0.18)
    return jnp.clip(spiked(values, jax.random.fold_in(stream_key, 3), *heavy), -limit, limit).astype(kind)


def setup_inputs(seed: int = 0) -> dict:
    splits = jax.random.split(jax.random.key(seed), 12)
    pet_image = jnp.clip(jnp.exp(math.log(2.0) - 1.3862944 * jax.random.uniform(splits[0], (NZ, NXW, Y_CELLS), jnp.float32) ** block_levels(splits[0], (NZ, NXW, Y_CELLS), ((0, 16),), -0.2, 0.2)), 0.5, 2.0)
    mr_image = bell_draw(splits[1], (NZ, NXW, 2 * Y_CELLS), 1.0, 6.0, ((0, 16),), jnp.float32)
    coil_sens = noise_with(splits[2], (COILS, NZ, NXW, 2 * Y_CELLS), 0.15, 0.8984375, ((0, 16), (1, 16)), (0, 2, 16, 2.0))
    kspace_data = bell_draw(splits[3], (COILS, NZ, NXW, 2 * Y_CELLS), 0.2, 1.1953125, ((0, 16), (2, 16)))
    kspace_mask = set_ends((jax.random.randint(splits[4], (NZ, Y_CELLS), 0, 2) < 1).astype(jnp.int32), jax.random.fold_in(splits[4], 1), 0, 1)
    system_tiles = jnp.clip(jnp.exp(math.log(4.0) - 5.996605 * jax.random.uniform(splits[5], (TILES, BLOCK_BINS, Y_CELLS), jnp.float32) ** block_levels(splits[5], (TILES, BLOCK_BINS, Y_CELLS), ((0, 256),), -0.2, 0.2)), 0.0099487305, 4.0).astype(jnp.bfloat16)
    tile_subset_block = set_ends(jax.random.randint(splits[6], (TILES,), 0, SUBSET_BLOCKS), jax.random.fold_in(splits[6], 1), 0, SUBSET_BLOCKS - 1).astype(jnp.int32)
    tile_col = set_ends(jax.random.randint(splits[7], (TILES,), 0, ZS * NXW), jax.random.fold_in(splits[7], 1), 0, (ZS * NXW) - 1).astype(jnp.int32)
    measured = jnp.clip(24.0 * jax.random.uniform(splits[8], (N_GRP * VIEWSET_BLOCKS, BLOCK_BINS), jnp.float32) ** block_levels(splits[8], (N_GRP * VIEWSET_BLOCKS, BLOCK_BINS), ((0, 16),), -0.2, 0.2), 0.0, 24.0)
    background = jnp.clip(jnp.exp(math.log(2.0) - 1.3862944 * jax.random.uniform(splits[9], (N_GRP * VIEWSET_BLOCKS, BLOCK_BINS), jnp.float32) ** block_levels(splits[9], (N_GRP * VIEWSET_BLOCKS, BLOCK_BINS), ((0, 16),), -0.2, 0.2)), 0.5, 2.0)
    subset_view_blocks = set_ends(jax.random.randint(splits[10], (N_GRP * SUBSET_BLOCKS,), 0, VIEWSET_BLOCKS), jax.random.fold_in(splits[10], 1), 0, VIEWSET_BLOCKS - 1).astype(jnp.int32)
    return {"pet_image": pet_image, "mr_image": mr_image, "coil_sens": coil_sens, "kspace_data": kspace_data, "kspace_mask": kspace_mask, "system_tiles": system_tiles, "tile_subset_block": tile_subset_block, "tile_col": tile_col, "measured": measured, "background": background, "subset_view_blocks": subset_view_blocks}


coupling_weight = 0.1
mag_smooth = 0.3
eta_smooth = 0.3

def dft_parts(length):
    indices = jnp.arange(length, dtype=jnp.int32)
    product = indices[:, None] * indices[None, :] % length
    angles = product.astype(jnp.float32) * (2.0 * math.pi / length)
    scaling = 1.0 / math.sqrt(length)
    return ((jnp.cos(angles) * scaling).astype(jnp.bfloat16), (-jnp.sin(angles) * scaling).astype(jnp.bfloat16))

def y_table(length):
    real_part, imag_part = dft_parts(length)
    upper_half = jnp.concatenate([real_part, imag_part], 1)
    lower_half = jnp.concatenate([-imag_part, real_part], 1)
    return jnp.concatenate([upper_half, lower_half], 0)

def z_table(length):
    real_part, imag_part = dft_parts(length)
    return jnp.concatenate([real_part, imag_part], 0)

def complex_mul(left_part, right_part, width):
    left_re, left_im = (left_part[..., :width], left_part[..., width:])
    right_re, right_im = (right_part[..., :width], right_part[..., width:])
    return jnp.concatenate([left_re * right_re - left_im * right_im, left_re * right_im + left_im * right_re], -1)

def complex_mul_conj(left_part, right_part, width):
    left_re, left_im = (left_part[..., :width], left_part[..., width:])
    right_re, right_im = (right_part[..., :width], right_part[..., width:])
    return jnp.concatenate([left_re * right_re + left_im * right_im, left_re * right_im - left_im * right_re], -1)

def z_apply(dft_table, volume, depth, width, inverse):
    product = jnp.einsum('kz,czxn->ckxn', dft_table.astype(jnp.float32), volume.astype(jnp.float32))
    upper_half, lower_half = (product[:, :depth], product[:, depth:])
    if inverse:
        real_part = upper_half[..., :width] + lower_half[..., width:]
        imag_part = upper_half[..., width:] - lower_half[..., :width]
    else:
        real_part = upper_half[..., :width] - lower_half[..., width:]
        imag_part = upper_half[..., width:] + lower_half[..., :width]
    return jnp.concatenate([real_part, imag_part], -1)

def forward_diff(volume, dim_index):
    extent = volume.shape[dim_index]
    ahead_part = lax.slice_in_dim(volume, 1, extent, axis=dim_index)
    here_part = lax.slice_in_dim(volume, 0, extent - 1, axis=dim_index)
    closing = jnp.zeros_like(lax.slice_in_dim(volume, 0, 1, axis=dim_index))
    return jnp.concatenate([ahead_part - here_part, closing], dim_index)

def coupling_sum(pet_values, mr_values):
    width = pet_values.shape[-1]
    magnitude = jnp.sqrt(mr_values[..., :width] ** 2 + mr_values[..., width:] ** 2 + mag_smooth ** 2)
    pet_diffs = [forward_diff(pet_values, dim_index) for dim_index in range(3)]
    mag_diffs = [forward_diff(magnitude, dim_index) for dim_index in range(3)]
    pet_sq = pet_diffs[0] ** 2 + pet_diffs[1] ** 2 + pet_diffs[2] ** 2
    mag_sq = mag_diffs[0] ** 2 + mag_diffs[1] ** 2 + mag_diffs[2] ** 2
    cross = pet_diffs[0] * mag_diffs[0] + pet_diffs[1] * mag_diffs[1] + pet_diffs[2] * mag_diffs[2]
    level_terms = jnp.sqrt(eta_smooth ** 2 + pet_sq * mag_sq - cross * cross)
    return jnp.sum(level_terms)

def reference(pet_image, mr_image, coil_sens, kspace_data, kspace_mask, system_tiles, tile_subset_block, tile_col, measured, background, subset_view_blocks):
    ky_table = y_table(Y_CELLS)
    kz_table = z_table(NZ)
    mask_float = kspace_mask.astype(jnp.float32)
    mask_wide = jnp.concatenate([mask_float, mask_float], -1)[:, None, :]

    def coil_term(running, coil_pack):
        sens_one, data_one = coil_pack
        sens_float = sens_one.astype(jnp.float32)
        coil_image = complex_mul(sens_float, mr_image, Y_CELLS).astype(jnp.bfloat16)
        ky_image = jnp.dot(coil_image.reshape(-1, 2 * Y_CELLS), ky_table, preferred_element_type=jnp.float32)
        ky_image = ky_image.astype(jnp.bfloat16).reshape(NZ, NXW, 2 * Y_CELLS)
        kspace = z_apply(kz_table, ky_image[None], NZ, Y_CELLS, False)[0]
        misfit = (mask_wide * (kspace - data_one.astype(jnp.float32))).astype(jnp.bfloat16)
        z_back = z_apply(kz_table, misfit[None], NZ, Y_CELLS, True)[0].astype(jnp.bfloat16)
        image_back = jnp.dot(z_back.reshape(-1, 2 * Y_CELLS), ky_table.T, preferred_element_type=jnp.float32)
        image_back = image_back.reshape(NZ, NXW, 2 * Y_CELLS)
        return (running + complex_mul_conj(sens_float, image_back, Y_CELLS), None)
    mr_fit, unused = lax.scan(coil_term, jnp.zeros((NZ, NXW, 2 * Y_CELLS), jnp.float32), (coil_sens, kspace_data))
    rows_all = NZ * NXW
    pet_rows = pet_image.astype(jnp.bfloat16).reshape(rows_all, Y_CELLS)
    tile_ids = jnp.arange(TILES, dtype=jnp.int32)
    slab_of = tile_ids // TPD % N_GZ
    voxel_row_index = (slab_of * (ZS * NXW) + tile_col).astype(jnp.int32)
    group_amounts = TPD * N_GZ

    def group_term(running, group_bundle):
        tile_bin_block, voxel_lookup, block_lookup, measurement_rows, backprojected_rows, view_numbers = group_bundle
        tiles_float = tile_bin_block.astype(jnp.float32)
        picked = jnp.take(pet_rows, voxel_lookup, axis=0).astype(jnp.float32)
        projected = jnp.einsum('kbn,kn->kb', tiles_float, picked)
        projection = jax.ops.segment_sum(projected, block_lookup, num_segments=SUBSET_BLOCKS) / Y_CELLS
        selected_counts = jnp.take(measurement_rows, view_numbers, axis=0)
        back_sel = jnp.take(backprojected_rows, view_numbers, axis=0)
        ratio = (1.0 - selected_counts / (projection + back_sel)).astype(jnp.bfloat16)
        ratio_tiles = jnp.take(ratio, block_lookup, axis=0).astype(jnp.float32)
        spread = jnp.einsum('kbn,kb->kn', tiles_float, ratio_tiles)
        return (running + jax.ops.segment_sum(spread, voxel_lookup, num_segments=rows_all), None)
    group_bundle = (system_tiles.reshape(N_GRP, group_amounts, BLOCK_BINS, Y_CELLS), voxel_row_index.reshape(N_GRP, group_amounts), tile_subset_block.reshape(N_GRP, group_amounts), measured.reshape(N_GRP, VIEWSET_BLOCKS, BLOCK_BINS), background.reshape(N_GRP, VIEWSET_BLOCKS, BLOCK_BINS), subset_view_blocks.reshape(N_GRP, SUBSET_BLOCKS))
    accum_rows, unused = lax.scan(group_term, jnp.zeros((rows_all, Y_CELLS), jnp.float32), group_bundle)
    pet_fit = (accum_rows / Y_CELLS).reshape(NZ, NXW, Y_CELLS)
    couple_pet, couple_mr = jax.grad(coupling_sum, argnums=(0, 1))(pet_image, mr_image)
    grad_pet = pet_fit + coupling_weight * couple_pet
    grad_mr = mr_fit + coupling_weight * couple_mr
    return (grad_pet, grad_mr)
```

```python
import math

import jax
import jax.numpy as jnp
import numpy as np
from jax import lax
from jax.experimental import pallas as pl
from jax.experimental.pallas import tpu as pltpu
from jax.sharding import Mesh, PartitionSpec as P

coupling_weight = 0.1
mag_smooth = 0.3
eta_smooth = 0.3

ZS, NX, NY, NZ = 8, 32, 480, 128
HALF = 512
ROW = 2 * HALF
CHUNK = ROW + HALF // 2
GRP = ("zh", "x", "c")
GZ = ("zl", "y")
f32, bf16 = jnp.float32, jnp.bfloat16

SMEM = pl.BlockSpec(memory_space=pltpu.SMEM)
VMEM = pl.BlockSpec(memory_space=pltpu.VMEM)


def dft_parts(length):
    indices = np.arange(length)
    angles = (indices[:, None] * indices[None, :] % length) * (2.0 * math.pi / length)
    scaling = 1.0 / math.sqrt(length)
    return np.cos(angles) * scaling, -np.sin(angles) * scaling


def y_table():
    real_part, imag_part = dft_parts(NY)
    table = np.zeros((2, HALF, 2, HALF), np.float64)
    table[0, :NY, 0, :NY] = real_part
    table[0, :NY, 1, :NY] = imag_part
    table[1, :NY, 0, :NY] = -imag_part
    table[1, :NY, 1, :NY] = real_part
    return jnp.asarray(table.reshape(ROW, ROW).astype(jnp.bfloat16))


def z_table():
    real_part, imag_part = dft_parts(NZ)
    table = np.block([[real_part, -imag_part], [imag_part, real_part]])
    return jnp.asarray(table.astype(jnp.bfloat16))


def call(kernel, out_shape, in_specs, scratch, flops, moved, name):
    return pl.pallas_call(
        kernel,
        out_shape=out_shape,
        in_specs=in_specs,
        out_specs=jax.tree.map(lambda _: VMEM, out_shape),
        scratch_shapes=scratch,
        compiler_params=pltpu.CompilerParams(vmem_limit_bytes=40 * 1024 * 1024),
        cost_estimate=pl.CostEstimate(flops=flops, bytes_accessed=moved, transcendentals=0),
        name=name,
    )


def pack_kernel(core_ref, sens_ref, mr_ref, out_ref, sens_rows, mr_rows):
    imag = core_ref[0] == 1
    last = NY - 3 * 128
    for part in range(2):
        sens_rows[4 * part + 3, :, last:] = jnp.zeros((2 * ZS * NX, 128 - last), f32)
    mr_rows[3, :, last:] = jnp.zeros((ZS * NX, 128 - last), f32)
    for q in range(2 * ZS):
        rows = pl.ds(q * NX, NX)
        for part in range(2):
            values = sens_ref[rows, part * NY : (part + 1) * NY].astype(f32)
            for b in range(4):
                block = values[:, 128 * b : min(128 * (b + 1), NY)]
                sens_rows[4 * part + b, rows, : block.shape[1]] = block
    for q in range(ZS):
        rows = pl.ds(q * NX, NX)
        values = jnp.where(imag, mr_ref[rows, NY:], mr_ref[rows, :NY])
        for b in range(4):
            block = values[:, 128 * b : min(128 * (b + 1), NY)]
            mr_rows[b, rows, : block.shape[1]] = block
    for x in range(NX):
        place = (x % 2) * (NX // 2) + x // 2
        for b in range(8):
            block = sens_rows[b, pl.ds(x, 2 * ZS, stride=NX), :]
            out_ref[place, :, 128 * b : 128 * (b + 1)] = block.astype(bf16)
        for b in range(2):
            block = jnp.concatenate(
                [mr_rows[b, pl.ds(x, ZS, stride=NX), :], mr_rows[b + 2, pl.ds(x, ZS, stride=NX), :]], 0
            )
            out_ref[place, :, ROW + 128 * b : ROW + 128 * (b + 1)] = block.astype(bf16)


def project_kernel(
    col_ref, block_ref, xs_ref, pet_ref, mr_ref, tiles_ref,
    bins_ref, win_ref, low_ref, high_ref, picked,
):
    for t in range(16):
        picked[pl.ds(t, 1), :] = pet_ref[pl.ds(col_ref[t], 1), :]
    rows = picked[...].astype(bf16)
    bins_ref[...] = jnp.zeros((16, 128), f32)
    for t in range(16):
        product = lax.dot_general(
            rows, tiles_ref[t], (((1,), (1,)), ((), ())), preferred_element_type=f32
        )
        place = pl.ds(block_ref[t], 1)
        bins_ref[place, :] = bins_ref[place, :] + product[t : t + 1, :]
    win_ref[...] = jnp.zeros((12, ZS, HALF), f32)
    low_ref[...] = jnp.zeros((16, HALF), f32)
    high_ref[...] = jnp.zeros((16, HALF), f32)
    for r in range(4):
        for z in range(ZS):
            place = pl.ds(xs_ref[r] + z * NX, 1)
            win_ref[r, z : z + 1, :NY] = pet_ref[place, :]
            win_ref[4 + r, z : z + 1, :NY] = mr_ref[place, :NY]
            win_ref[8 + r, z : z + 1, :NY] = mr_ref[place, NY:]
    for r in range(12):
        low_ref[pl.ds(r, 1), :] = win_ref[r, 0:1, :]
        high_ref[pl.ds(r, 1), :] = win_ref[r, ZS - 1 : ZS, :]


def backproject_kernel(
    col_ref, block_ref, view_ref, bins_ref, measured_ref, background_ref, tiles_ref,
    out_ref, ratio, gathered, acc,
):
    for j in range(16):
        counts = measured_ref[pl.ds(view_ref[j], 1), :]
        back = background_ref[pl.ds(view_ref[j], 1), :]
        projection = bins_ref[j : j + 1, :] / NY
        ratio[j : j + 1, :] = 1.0 - counts / (projection + back)
    for t in range(16):
        gathered[t : t + 1, :] = ratio[pl.ds(block_ref[t], 1), :]
    rows = gathered[...].astype(bf16)
    acc[...] = jnp.zeros((4, ZS * NX, 128), f32)
    for t in range(16):
        spread = jnp.dot(rows, tiles_ref[t], preferred_element_type=f32)
        place = pl.ds(col_ref[t], 1)
        for b in range(4):
            block = spread[t : t + 1, 128 * b : min(128 * (b + 1), NY)]
            lanes = slice(0, block.shape[1])
            acc[b, place, lanes] = acc[b, place, lanes] + block
    for p in range(16):
        for k in range(2):
            for b in range(4):
                block = acc[b, pl.ds(2 * p + k, ZS, stride=NX), :] / NY
                first = k * HALF + 128 * b
                out_ref[p, :, first : first + 128] = block.astype(bf16)


def coupling_kernel(
    info_ref, win_ref, prev_ref, next_ref, pet_out, mr_out, planes, mags, moved
):
    z_start, x_first = info_ref[0], info_ref[1]
    planes[...] = jnp.zeros((12, 24, HALF), f32)
    for r in range(12):
        planes[r, 0:1, :] = prev_ref[r : r + 1, :]
        planes[r, 1 : ZS + 1, :] = win_ref[r]
        planes[r, ZS + 1 : ZS + 2, :] = next_ref[r : r + 1, :]
    for r in range(4):
        mags[r] = jnp.sqrt(planes[4 + r] ** 2 + planes[8 + r] ** 2 + mag_smooth**2)
    shape = (16, HALF)
    level = z_start - 1 + lax.broadcasted_iota(jnp.int32, shape, 0)
    lane = lax.broadcasted_iota(jnp.int32, shape, 1)
    step_z = level < NZ - 1
    step_y = lane < NY - 1
    term_z = (level >= 0) & (lane < NY)

    def differences(ref, r, step_x):
        here = ref[r, 0:16, :]
        along_z = jnp.where(step_z, ref[r, 1:17, :] - here, 0.0)
        along_x = jnp.where(step_x, ref[r + 1, 0:16, :] - here, 0.0)
        along_y = jnp.where(step_y, pltpu.roll(here, HALF - 1, 1) - here, 0.0)
        return along_z, along_x, along_y

    grads = []
    for r in range(3):
        place = x_first - 1 + r
        step_x = place < NX - 1
        a = differences(planes, r, step_x)
        b = differences(mags, r, step_x)
        a_sq = a[0] ** 2 + a[1] ** 2 + a[2] ** 2
        b_sq = b[0] ** 2 + b[1] ** 2 + b[2] ** 2
        cross = a[0] * b[0] + a[1] * b[1] + a[2] * b[2]
        weight = lax.rsqrt(eta_smooth**2 + a_sq * b_sq - cross * cross)
        weight = jnp.where(term_z & (place >= 0), weight, 0.0)
        grads.append(
            (
                [(p * b_sq - q * cross) * weight for p, q in zip(a, b)],
                [(q * a_sq - p * cross) * weight for p, q in zip(a, b)],
            )
        )

    for k in range(2):
        found = []
        for which in range(2):
            here, before = grads[k + 1][which], grads[k][which]
            total = before[1] - here[0] - here[1] - here[2]
            total = total + pltpu.roll(here[0], 1, 0) + pltpu.roll(here[2], 1, 1)
            found.append(coupling_weight * total)
        moved[0] = found[0]
        scaled = found[1] / mags[k + 1, 0:16, :]
        moved[1] = scaled * planes[5 + k, 0:16, :]
        moved[2] = scaled * planes[9 + k, 0:16, :]
        pet_out[k] = moved[0, 1 : ZS + 1, :]
        mr_out[k, :, :HALF] = moved[1, 1 : ZS + 1, :]
        mr_out[k, :, HALF:] = moved[2, 1 : ZS + 1, :]


def coil_kernel(recv_ref, data_own_ref, data_got_ref, mask_ref, ytab_ref, ztab_ref, core_ref,
                out_ref, sens, images, kyrows):
    def image_part(c):
        part = recv_ref[c * 16 : (c + 1) * 16, :, ROW:].astype(f32)
        left = part[:, :ZS].reshape(NZ, HALF // 2)
        right = part[:, ZS:].reshape(NZ, HALF // 2)
        return jnp.concatenate([left, right], -1)

    mr_re, mr_im = image_part(0), image_part(1)
    for c in range(2):
        block = recv_ref[c * 16 : (c + 1) * 16, :, :ROW].astype(f32)
        for k in range(2):
            q = 2 * c + k
            rows = pl.ds(q * NZ, NZ)
            one = block[:, k * ZS : (k + 1) * ZS].reshape(NZ, ROW)
            s_re, s_im = one[:, :HALF], one[:, HALF:]
            sens[rows, :] = one
            images[rows, :HALF] = (s_re * mr_re - s_im * mr_im).astype(bf16)
            images[rows, HALF:] = (s_re * mr_im + s_im * mr_re).astype(bf16)
    kyrows[...] = jnp.dot(images[...], ytab_ref[...], preferred_element_type=f32).astype(bf16)
    mask = mask_ref[...].astype(f32)
    on_first = core_ref[0] == 0
    ztab = ztab_ref[...]
    for q in range(4):
        rows = pl.ds(q * NZ, NZ)
        volume = jnp.concatenate([kyrows[rows, :HALF], kyrows[rows, HALF:]], 0)
        kspace = jnp.dot(ztab, volume, preferred_element_type=f32)
        k = q % 2
        own_first = on_first if q < 2 else jnp.logical_not(on_first)
        data = jnp.where(own_first, data_own_ref[k].astype(f32), data_got_ref[k].astype(f32))
        misfit = jnp.concatenate(
            [mask * (kspace[:NZ] - data[:NZ]), mask * (data[NZ:] - kspace[NZ:])], 0
        ).astype(bf16)
        back = jnp.dot(ztab, misfit, preferred_element_type=f32).astype(bf16)
        images[rows, :HALF] = back[:NZ]
        images[rows, HALF:] = back[NZ:]
    total_re = jnp.zeros((NZ, HALF), f32)
    total_im = jnp.zeros((NZ, HALF), f32)
    for q in range(4):
        rows = pl.ds(q * NZ, NZ)
        image = jnp.dot(images[rows, :], ytab_ref[...], preferred_element_type=f32)
        i_re, i_im = image[:, :HALF], image[:, HALF:]
        s_re, s_im = sens[rows, :HALF], sens[rows, HALF:]
        total_re = total_re + (s_re * i_re - s_im * i_im)
        total_im = total_im - (s_re * i_im + s_im * i_re)
    out_ref[:, :, :HALF] = total_re.reshape(16, ZS, HALF).astype(bf16)
    out_ref[:, :, HALF:] = total_im.reshape(16, ZS, HALF).astype(bf16)


def sum_kernel(recv_ref, mr_out, pet_out):
    pet = jnp.zeros((ZS, ROW), f32)
    for c in range(2):
        mr = jnp.zeros((ZS, ROW), f32)
        for g in range(8):
            block = recv_ref[2 * g + c].astype(f32)
            mr = mr + block[:ZS]
            pet = pet + block[ZS:]
        mr_out[c * ZS : (c + 1) * ZS, :] = mr
    pet_out[...] = pet


def final_kernel(mr_ref, pet_ref, couple_pet_ref, couple_mr_ref, pet_out, mr_out):
    for k in range(2):
        rows = pl.ds(k * ZS, ZS)
        pet = pet_ref[:, k * HALF : (k + 1) * HALF] + couple_pet_ref[k]
        mr = mr_ref[rows, :] + couple_mr_ref[k]
        pet_out[:, k, :] = pet[:, :NY]
        mr_out[:, k, :NY] = mr[:, :NY]
        mr_out[:, k, NY:] = mr[:, HALF : HALF + NY]


def sds(shape, dtype):
    return jax.ShapeDtypeStruct(shape, dtype)


def on_device(
    pet_image, mr_image, coil_sens, kspace_data, kspace_mask, system_tiles,
    tile_subset_block, tile_col, measured, background, subset_view_blocks,
):
    core = lax.axis_index("c")
    grp = lax.axis_index(GRP)
    gz = lax.axis_index(GZ)
    core_arr = core.astype(jnp.int32).reshape(1)
    pet_rows = pet_image.reshape(ZS * NX, NY)
    mr_rows = mr_image.reshape(ZS * NX, 2 * NY)

    sent = call(
        pack_kernel, sds((32, 16, CHUNK), bf16), [SMEM, VMEM, VMEM],
        [pltpu.VMEM((8, 2 * ZS * NX, 128), f32), pltpu.VMEM((4, ZS * NX, 128), f32)],
        10**6, 4 * 10**6, "pack",
    )(core_arr, coil_sens.reshape(2 * ZS * NX, 2 * NY), mr_rows)
    recv = lax.all_to_all(sent, ("c",) + GZ, split_axis=0, concat_axis=0, tiled=True)

    data = kspace_data.reshape(2, NZ, 2, 2, NY).transpose(2, 0, 3, 1, 4)
    data = jnp.pad(data, ((0, 0),) * 4 + ((0, HALF - NY),)).reshape(2, 2, 2 * NZ, HALF)
    data_own = lax.dynamic_index_in_dim(data, core, 0, keepdims=False)
    data_out = lax.dynamic_index_in_dim(data, 1 - core, 0, keepdims=False)
    data_got = lax.ppermute(data_out, "c", [(0, 1), (1, 0)])
    mask = jnp.pad(kspace_mask, ((0, 0), (0, HALF - NY)))

    xs = jnp.clip(2 * grp - 1 + jnp.arange(4, dtype=jnp.int32), 0, NX - 1)
    bins, win, low, high = call(
        project_kernel,
        (sds((16, 128), f32), sds((12, ZS, HALF), f32), sds((16, HALF), f32), sds((16, HALF), f32)),
        [SMEM, SMEM, SMEM, VMEM, VMEM, VMEM],
        [pltpu.VMEM((16, NY), f32)],
        10**7, 4 * 10**6, "project",
    )(tile_col, tile_subset_block, xs, pet_rows, mr_rows, system_tiles)
    from_prev = lax.ppermute(high, GZ, [(i, i + 1) for i in range(15)])
    from_next = lax.ppermute(low, GZ, [(i + 1, i) for i in range(15)])
    for k in (1, 2, 4, 8):
        bins = bins + lax.ppermute(bins, GZ, [(i, i ^ k) for i in range(16)])
    pet_part = call(
        backproject_kernel, sds((16, ZS, ROW), bf16), [SMEM, SMEM, SMEM, VMEM, VMEM, VMEM, VMEM],
        [pltpu.VMEM((16, 128), f32), pltpu.VMEM((16, 128), f32), pltpu.VMEM((4, ZS * NX, 128), f32)],
        10**7, 3 * 10**6, "backproject",
    )(tile_col, tile_subset_block, subset_view_blocks, bins, measured, background, system_tiles)
    info = jnp.stack([gz * ZS, 2 * grp]).astype(jnp.int32)
    couple_pet, couple_mr = call(
        coupling_kernel, (sds((2, ZS, HALF), f32), sds((2, ZS, ROW), f32)),
        [SMEM, VMEM, VMEM, VMEM],
        [pltpu.VMEM((12, 24, HALF), f32), pltpu.VMEM((4, 24, HALF), f32),
         pltpu.VMEM((3, 16, HALF), f32)],
        10**6, 10**6, "coupling",
    )(info, win, from_prev, from_next)

    mr_part = call(
        coil_kernel, sds((16, ZS, ROW), bf16), [VMEM] * 6 + [SMEM],
        [pltpu.VMEM((4 * NZ, ROW), f32), pltpu.VMEM((4 * NZ, ROW), bf16),
         pltpu.VMEM((4 * NZ, ROW), bf16)],
        5 * 10**9, 6 * 10**6, "coils",
    )(recv, data_own, data_got, mask, y_table(), z_table(), core_arr)

    both = lax.all_to_all(
        jnp.concatenate([mr_part, pet_part], 1), GRP, split_axis=0, concat_axis=0, tiled=True
    )
    mr_sum, pet_sum = call(
        sum_kernel, (sds((2 * ZS, ROW), f32), sds((ZS, ROW), f32)), [VMEM], [],
        10**6, 10**6, "sums",
    )(both)
    mr_here = lax.ppermute(
        mr_sum, GRP + GZ, [(g * 16 + j, j * 16 + g) for g in range(16) for j in range(16)]
    )
    return call(
        final_kernel, (sds((ZS, 2, NY), f32), sds((ZS, 2, 2 * NY), f32)), [VMEM] * 4, [],
        10**5, 10**6, "final",
    )(mr_here, pet_sum, couple_pet, couple_mr)


def solution(mesh):
    fine = Mesh(mesh.devices.reshape(2, 4, 2, 4, 4), ("zh", "x", "c", "zl", "y"))
    placed = (
        P(GZ, None, None),
        P(GZ, None, None),
        P(GRP, GZ, None, None),
        P(GRP, None, GZ, None),
        P(),
        P(GRP + GZ, None, None),
        P(GRP + GZ),
        P(GRP + GZ),
        P(GRP, None),
        P(GRP, None),
        P(GRP),
    )
    return jax.shard_map(
        on_device,
        mesh=fine,
        in_specs=placed,
        out_specs=(P(GZ, GRP, None), P(GZ, GRP, None)),
        check_vma=False,
    )
```

```python
import math

import jax
import jax.numpy as jnp
import numpy as np
from jax import lax
from jax.experimental import pallas as pl
from jax.experimental.pallas import tpu as pltpu
from jax.sharding import Mesh, PartitionSpec as P

coupling_weight = 0.1
mag_smooth = 0.3
eta_smooth = 0.3

ZS, NX, NY, NZ = 8, 32, 480, 128
HALF = 512
ROW = 2 * HALF
CHUNK = ROW + HALF // 2
GRP = ("zh", "x", "c")
GZ = ("zl", "y")
f32, bf16 = jnp.float32, jnp.bfloat16

SMEM = pl.BlockSpec(memory_space=pltpu.SMEM)
VMEM = pl.BlockSpec(memory_space=pltpu.VMEM)
HBM = pl.BlockSpec(memory_space=pltpu.HBM)


def dft_parts(length):
    indices = np.arange(length)
    angles = (indices[:, None] * indices[None, :] % length) * (2.0 * math.pi / length)
    scaling = 1.0 / math.sqrt(length)
    return np.cos(angles) * scaling, -np.sin(angles) * scaling


def y_table():
    real_part, imag_part = dft_parts(NY)
    table = np.zeros((2, HALF, 2, HALF), np.float64)
    table[0, :NY, 0, :NY] = real_part
    table[0, :NY, 1, :NY] = imag_part
    table[1, :NY, 0, :NY] = -imag_part
    table[1, :NY, 1, :NY] = real_part
    return jnp.asarray(table.reshape(ROW, ROW).astype(jnp.bfloat16))


def z_table():
    real_part, imag_part = dft_parts(NZ)
    table = np.block([[real_part, -imag_part], [imag_part, real_part]])
    return jnp.asarray(table.astype(jnp.bfloat16))


def call(kernel, out_shape, in_specs, scratch, flops, moved, name, out_spec=VMEM, grant=40):
    return pl.pallas_call(
        kernel,
        out_shape=out_shape,
        in_specs=in_specs,
        out_specs=jax.tree.map(lambda _: out_spec, out_shape),
        scratch_shapes=scratch,
        compiler_params=pltpu.CompilerParams(vmem_limit_bytes=grant * 1024 * 1024),
        cost_estimate=pl.CostEstimate(flops=flops, bytes_accessed=moved, transcendentals=0),
        name=name,
    )


def pack_kernel(core_ref, sens_hbm, mr_hbm, out_hbm, sens_ref, mr_ref, sens_rows, mr_rows, out_ref,
                sens_sems, mr_sems, out_sems):
    sens_copies = [
        pltpu.make_async_copy(sens_hbm.at[pl.ds(128 * n, 128)], sens_ref.at[pl.ds(128 * n, 128)], sens_sems.at[n])
        for n in range(4)
    ]
    mr_copies = [
        pltpu.make_async_copy(mr_hbm.at[pl.ds(128 * n, 128)], mr_ref.at[pl.ds(128 * n, 128)], mr_sems.at[n])
        for n in range(2)
    ]
    for copy in sens_copies + mr_copies:
        copy.start()
    imag = core_ref[0] == 1
    last = NY - 3 * 128
    for part in range(2):
        sens_rows[4 * part + 3, :, last:] = jnp.zeros((2 * ZS * NX, 128 - last), f32)
    mr_rows[3, :, last:] = jnp.zeros((ZS * NX, 128 - last), f32)
    for q in range(2 * ZS):
        if q % 4 == 0:
            sens_copies[q // 4].wait()
        rows = pl.ds(q * NX, NX)
        for part in range(2):
            values = sens_ref[rows, part * NY : (part + 1) * NY].astype(f32)
            for b in range(4):
                block = values[:, 128 * b : min(128 * (b + 1), NY)]
                sens_rows[4 * part + b, rows, : block.shape[1]] = block
    for q in range(ZS):
        if q % 4 == 0:
            mr_copies[q // 4].wait()
        rows = pl.ds(q * NX, NX)
        values = jnp.where(imag, mr_ref[rows, NY:], mr_ref[rows, :NY])
        for b in range(4):
            block = values[:, 128 * b : min(128 * (b + 1), NY)]
            mr_rows[b, rows, : block.shape[1]] = block
    out_copies = []
    for place in range(NX):
        x = 2 * (place % 16) + place // 16
        for b in range(8):
            block = sens_rows[b, pl.ds(x, 2 * ZS, stride=NX), :]
            out_ref[place, :, 128 * b : 128 * (b + 1)] = block.astype(bf16)
        for b in range(2):
            block = jnp.concatenate(
                [mr_rows[b, pl.ds(x, ZS, stride=NX), :], mr_rows[b + 2, pl.ds(x, ZS, stride=NX), :]], 0
            )
            out_ref[place, :, ROW + 128 * b : ROW + 128 * (b + 1)] = block.astype(bf16)
        if place % 4 == 3:
            part = pl.ds(place - 3, 4)
            copy = pltpu.make_async_copy(out_ref.at[part], out_hbm.at[part], out_sems.at[place // 4])
            copy.start()
            out_copies.append(copy)
    for copy in out_copies:
        copy.wait()


def project_kernel(
    col_ref, block_ref, xs_ref, pet_ref, mr_ref, tiles_ref,
    bins_ref, win_ref, low_ref, high_ref, picked,
):
    for t in range(16):
        picked[pl.ds(t, 1), :] = pet_ref[pl.ds(col_ref[t], 1), :]
    rows = picked[...].astype(bf16)
    bins_ref[...] = jnp.zeros((16, 128), f32)
    for t in range(16):
        product = jnp.dot(rows, tiles_ref[t], preferred_element_type=f32)
        place = pl.ds(block_ref[t], 1)
        bins_ref[place, :] = bins_ref[place, :] + product[t : t + 1, :]
    win_ref[...] = jnp.zeros((12, ZS, HALF), f32)
    low_ref[...] = jnp.zeros((16, HALF), f32)
    high_ref[...] = jnp.zeros((16, HALF), f32)
    for r in range(4):
        for z in range(ZS):
            place = pl.ds(xs_ref[r] + z * NX, 1)
            win_ref[r, z : z + 1, :NY] = pet_ref[place, :]
            win_ref[4 + r, z : z + 1, :NY] = mr_ref[place, :NY]
            win_ref[8 + r, z : z + 1, :NY] = mr_ref[place, NY:]
    for r in range(12):
        low_ref[pl.ds(r, 1), :] = win_ref[r, 0:1, :]
        high_ref[pl.ds(r, 1), :] = win_ref[r, ZS - 1 : ZS, :]


def backproject_kernel(
    col_ref, block_ref, view_ref, bins_ref, measured_ref, background_ref, tiles_ref,
    out_ref, ratio, gathered, acc,
):
    for j in range(16):
        counts = measured_ref[pl.ds(view_ref[j], 1), :]
        back = background_ref[pl.ds(view_ref[j], 1), :]
        projection = bins_ref[j : j + 1, :] / NY
        ratio[j : j + 1, :] = 1.0 - counts / (projection + back)
    for t in range(16):
        gathered[t : t + 1, :] = ratio[pl.ds(block_ref[t], 1), :]
    rows = gathered[...].astype(bf16)
    acc[...] = jnp.zeros((4, ZS * NX, 128), f32)
    for t in range(16):
        spread = lax.dot_general(
            rows, tiles_ref[t], (((1,), (1,)), ((), ())), preferred_element_type=f32
        )
        place = pl.ds(col_ref[t], 1)
        for b in range(4):
            block = spread[t : t + 1, 128 * b : min(128 * (b + 1), NY)]
            lanes = slice(0, block.shape[1])
            acc[b, place, lanes] = acc[b, place, lanes] + block
    for p in range(16):
        for k in range(2):
            for b in range(4):
                block = acc[b, pl.ds(2 * p + k, ZS, stride=NX), :] / NY
                first = k * HALF + 128 * b
                rows = slice(p // 8 * ZS, (p // 8 + 1) * ZS)
                out_ref[p % 8, rows, first : first + 128] = block.astype(bf16)


def coupling_kernel(
    info_ref, win_ref, prev_ref, next_ref, pet_out, mr_out, planes, mags, moved
):
    z_start, x_first = info_ref[0], info_ref[1]
    planes[...] = jnp.zeros((12, 24, HALF), f32)
    for r in range(12):
        planes[r, 0:1, :] = prev_ref[r : r + 1, :]
        planes[r, 1 : ZS + 1, :] = win_ref[r]
        planes[r, ZS + 1 : ZS + 2, :] = next_ref[r : r + 1, :]
    for r in range(4):
        mags[r] = jnp.sqrt(planes[4 + r] ** 2 + planes[8 + r] ** 2 + mag_smooth**2)
    shape = (16, HALF)
    level = z_start - 1 + lax.broadcasted_iota(jnp.int32, shape, 0)
    lane = lax.broadcasted_iota(jnp.int32, shape, 1)
    step_z = level < NZ - 1
    step_y = lane < NY - 1
    term_z = (level >= 0) & (lane < NY)

    def differences(ref, r, step_x):
        here = ref[r, 0:16, :]
        along_z = jnp.where(step_z, ref[r, 1:17, :] - here, 0.0)
        along_x = jnp.where(step_x, ref[r + 1, 0:16, :] - here, 0.0)
        along_y = jnp.where(step_y, pltpu.roll(here, HALF - 1, 1) - here, 0.0)
        return along_z, along_x, along_y

    grads = []
    for r in range(3):
        place = x_first - 1 + r
        step_x = place < NX - 1
        a = differences(planes, r, step_x)
        b = differences(mags, r, step_x)
        a_sq = a[0] ** 2 + a[1] ** 2 + a[2] ** 2
        b_sq = b[0] ** 2 + b[1] ** 2 + b[2] ** 2
        cross = a[0] * b[0] + a[1] * b[1] + a[2] * b[2]
        weight = lax.rsqrt(eta_smooth**2 + a_sq * b_sq - cross * cross)
        weight = jnp.where(term_z & (place >= 0), weight, 0.0)
        grads.append(
            (
                [(p * b_sq - q * cross) * weight for p, q in zip(a, b)],
                [(q * a_sq - p * cross) * weight for p, q in zip(a, b)],
            )
        )

    for k in range(2):
        found = []
        for which in range(2):
            here, before = grads[k + 1][which], grads[k][which]
            total = before[1] - here[0] - here[1] - here[2]
            total = total + pltpu.roll(here[0], 1, 0) + pltpu.roll(here[2], 1, 1)
            found.append(coupling_weight * total)
        moved[0] = found[0]
        scaled = found[1] / mags[k + 1, 0:16, :]
        moved[1] = scaled * planes[5 + k, 0:16, :]
        moved[2] = scaled * planes[9 + k, 0:16, :]
        pet_out[k] = moved[0, 1 : ZS + 1, :]
        mr_out[k, :, :HALF] = moved[1, 1 : ZS + 1, :]
        mr_out[k, :, HALF:] = moved[2, 1 : ZS + 1, :]


def coil_kernel(core_ref, recv_hbm, ytab_hbm, data_own_ref, data_got_ref, mask_ref, ztab_ref, pet_ref,
                out_ref, recv_ref, ytab_ref, sens, images, kyrows, recv_sems, ytab_sems):
    def received(n, c, lanes):
        place = (pl.ds(16 * c, 16), slice(None), lanes)
        return pltpu.make_async_copy(recv_hbm.at[place], recv_ref.at[place], recv_sems.at[n])

    copies = [
        received(0, 0, pl.ds(ROW, HALF // 2)),
        received(1, 1, pl.ds(ROW, HALF // 2)),
        received(2, 0, pl.ds(0, ROW)),
        received(3, 1, pl.ds(0, ROW)),
    ]
    tables = [
        pltpu.make_async_copy(
            ytab_hbm.at[pl.ds(256 * n, 256)], ytab_ref.at[pl.ds(256 * n, 256)], ytab_sems.at[n]
        )
        for n in range(4)
    ]
    for copy in copies + tables:
        copy.start()
    out_ref[:, 2 * ZS :] = pet_ref[...]

    def image_part(c):
        part = recv_ref[c * 16 : (c + 1) * 16, :, ROW:].astype(f32)
        left = part[:, :ZS].reshape(NZ, HALF // 2)
        right = part[:, ZS:].reshape(NZ, HALF // 2)
        return jnp.concatenate([left, right], -1)

    copies[0].wait()
    copies[1].wait()
    mr_re, mr_im = image_part(0), image_part(1)
    mask = mask_ref[...].astype(f32)
    on_first = core_ref[0] == 0
    ztab = ztab_ref[...]
    for c in range(2):
        copies[2 + c].wait()
        block = recv_ref[c * 16 : (c + 1) * 16, :, :ROW].astype(f32)
        for k in range(2):
            rows = pl.ds((2 * c + k) * NZ, NZ)
            one = block[:, k * ZS : (k + 1) * ZS].reshape(NZ, ROW)
            s_re, s_im = one[:, :HALF], one[:, HALF:]
            sens[rows, :] = one
            images[rows, :HALF] = (s_re * mr_re - s_im * mr_im).astype(bf16)
            images[rows, HALF:] = (s_re * mr_im + s_im * mr_re).astype(bf16)
    for copy in tables:
        copy.wait()
    for c in range(2):
        pair = pl.ds(2 * c * NZ, 2 * NZ)
        kyrows[pair, :] = jnp.dot(images[pair, :], ytab_ref[...], preferred_element_type=f32).astype(bf16)
        own = on_first if c == 0 else jnp.logical_not(on_first)
        for k in range(2):
            rows = pl.ds((2 * c + k) * NZ, NZ)
            volume = jnp.concatenate([kyrows[rows, :HALF], kyrows[rows, HALF:]], 0)
            kspace = jnp.dot(ztab, volume, preferred_element_type=f32)
            data = jnp.where(own, data_own_ref[k].astype(f32), data_got_ref[k].astype(f32))
            misfit = jnp.concatenate(
                [mask * (kspace[:NZ] - data[:NZ]), mask * (data[NZ:] - kspace[NZ:])], 0
            ).astype(bf16)
            back = jnp.dot(ztab, misfit, preferred_element_type=f32).astype(bf16)
            images[rows, :HALF] = back[:NZ]
            images[rows, HALF:] = back[NZ:]
    total_re = jnp.zeros((NZ, HALF), f32)
    total_im = jnp.zeros((NZ, HALF), f32)
    for c in range(2):
        pair = pl.ds(2 * c * NZ, 2 * NZ)
        image = jnp.dot(images[pair, :], ytab_ref[...], preferred_element_type=f32)
        for k in range(2):
            rows = pl.ds((2 * c + k) * NZ, NZ)
            i_re, i_im = image[k * NZ : (k + 1) * NZ, :HALF], image[k * NZ : (k + 1) * NZ, HALF:]
            s_re, s_im = sens[rows, :HALF], sens[rows, HALF:]
            total_re = total_re + (s_re * i_re - s_im * i_im)
            total_im = total_im - (s_re * i_im + s_im * i_re)
    for part, total in enumerate((total_re, total_im)):
        slabs = total.reshape(2, 8, ZS, HALF)
        both = jnp.concatenate([slabs[0], slabs[1]], 1)
        out_ref[:, : 2 * ZS, part * HALF : (part + 1) * HALF] = both.astype(bf16)


def sum_kernel(half_ref, recv_ref, mr_own, mr_other, pet_own, pet_other):
    upper = half_ref[0] == 1
    pet = jnp.zeros((2 * ZS, ROW), f32)
    for c in range(2):
        mr = jnp.zeros((2 * ZS, ROW), f32)
        for x in range(4):
            block = recv_ref[2 * x + c].astype(f32)
            mr = mr + block[: 2 * ZS]
            pet = pet + block[2 * ZS :]
        rows = pl.ds(c * ZS, ZS)
        mr_own[rows, :] = jnp.where(upper, mr[ZS:], mr[:ZS])
        mr_other[rows, :] = jnp.where(upper, mr[:ZS], mr[ZS:])
    pet_own[...] = jnp.where(upper, pet[ZS:], pet[:ZS])
    pet_other[...] = jnp.where(upper, pet[:ZS], pet[ZS:])


def final_kernel(mr_a, mr_b, pet_a, pet_b, couple_pet_ref, couple_mr_ref, pet_out, mr_out):
    for k in range(2):
        rows = pl.ds(k * ZS, ZS)
        lanes = pl.ds(k * HALF, HALF)
        pet = pet_a[:, lanes] + pet_b[:, lanes] + couple_pet_ref[k]
        mr = mr_a[rows, :] + mr_b[rows, :] + couple_mr_ref[k]
        pet_out[:, k, :] = pet[:, :NY]
        mr_out[:, k, :NY] = mr[:, :NY]
        mr_out[:, k, NY:] = mr[:, HALF : HALF + NY]


def sds(shape, dtype):
    return jax.ShapeDtypeStruct(shape, dtype)


def on_device(
    pet_image, mr_image, coil_sens, kspace_data, kspace_mask, system_tiles,
    tile_subset_block, tile_col, measured, background, subset_view_blocks,
):
    core = lax.axis_index("c")
    grp = lax.axis_index(GRP)
    gz = lax.axis_index(GZ)
    core_arr = core.astype(jnp.int32).reshape(1)
    pet_rows = pet_image.reshape(ZS * NX, NY)
    mr_rows = mr_image.reshape(ZS * NX, 2 * NY)
    tiles = system_tiles.swapaxes(1, 2)

    sent = call(
        pack_kernel, sds((32, 16, CHUNK), bf16), [SMEM, HBM, HBM],
        [pltpu.VMEM((2 * ZS * NX, 2 * NY), bf16), pltpu.VMEM((ZS * NX, 2 * NY), f32),
         pltpu.VMEM((8, 2 * ZS * NX, 128), f32), pltpu.VMEM((4, ZS * NX, 128), f32),
         pltpu.VMEM((32, 16, CHUNK), bf16), pltpu.SemaphoreType.DMA((4,)),
         pltpu.SemaphoreType.DMA((2,)), pltpu.SemaphoreType.DMA((8,))],
        10**6, 4 * 10**6, "pack", HBM, 60,
    )(core_arr, coil_sens.reshape(2 * ZS * NX, 2 * NY), mr_rows)
    sent, tile_col = lax.optimization_barrier((sent, tile_col))
    recv = lax.all_to_all(sent, ("c",) + GZ, split_axis=0, concat_axis=0, tiled=True)

    data = kspace_data.reshape(2, NZ, 2, 2, NY).transpose(2, 0, 3, 1, 4)
    data = jnp.pad(data, ((0, 0),) * 4 + ((0, HALF - NY),)).reshape(2, 2, 2 * NZ, HALF)
    data_own = lax.dynamic_index_in_dim(data, core, 0, keepdims=False)
    data_out = lax.dynamic_index_in_dim(data, 1 - core, 0, keepdims=False)
    data_got = lax.ppermute(data_out, "c", [(0, 1), (1, 0)])
    mask = jnp.pad(kspace_mask, ((0, 0), (0, HALF - NY)))

    xs = jnp.clip(2 * grp - 1 + jnp.arange(4, dtype=jnp.int32), 0, NX - 1)
    bins, win, low, high = call(
        project_kernel,
        (sds((16, 128), f32), sds((12, ZS, HALF), f32), sds((16, HALF), f32), sds((16, HALF), f32)),
        [SMEM, SMEM, SMEM, VMEM, VMEM, VMEM],
        [pltpu.VMEM((16, NY), f32)],
        10**7, 4 * 10**6, "project",
    )(tile_col, tile_subset_block, xs, pet_rows, mr_rows, tiles)
    from_prev = lax.ppermute(high, GZ, [(i, i + 1) for i in range(15)])
    from_next = lax.ppermute(low, GZ, [(i + 1, i) for i in range(15)])
    for k in (1, 2, 4, 8):
        bins = bins + lax.ppermute(bins, GZ, [(i, i ^ k) for i in range(16)])
    pet_part = call(
        backproject_kernel, sds((8, 2 * ZS, ROW), bf16), [SMEM, SMEM, SMEM, VMEM, VMEM, VMEM, VMEM],
        [pltpu.VMEM((16, 128), f32), pltpu.VMEM((16, 128), f32), pltpu.VMEM((4, ZS * NX, 128), f32)],
        10**7, 3 * 10**6, "backproject",
    )(tile_col, tile_subset_block, subset_view_blocks, bins, measured, background, tiles)
    info = jnp.stack([gz * ZS, 2 * grp]).astype(jnp.int32)
    couple_pet, couple_mr = call(
        coupling_kernel, (sds((2, ZS, HALF), f32), sds((2, ZS, ROW), f32)),
        [SMEM, VMEM, VMEM, VMEM],
        [pltpu.VMEM((12, 24, HALF), f32), pltpu.VMEM((4, 24, HALF), f32),
         pltpu.VMEM((3, 16, HALF), f32)],
        10**6, 10**6, "coupling",
    )(info, win, from_prev, from_next)

    recv, pet_part, couple_pet, couple_mr = lax.optimization_barrier(
        (recv, pet_part, couple_pet, couple_mr)
    )
    parts = call(
        coil_kernel, sds((8, 4 * ZS, ROW), bf16), [SMEM, HBM, HBM] + [VMEM] * 5,
        [pltpu.VMEM((32, 16, CHUNK), bf16), pltpu.VMEM((ROW, ROW), bf16),
         pltpu.VMEM((4 * NZ, ROW), f32), pltpu.VMEM((4 * NZ, ROW), bf16),
         pltpu.VMEM((4 * NZ, ROW), bf16), pltpu.SemaphoreType.DMA((4,)), pltpu.SemaphoreType.DMA((4,))],
        5 * 10**9, 6 * 10**6, "coils",
    )(core_arr, recv, y_table(), data_own, data_got, mask, z_table(), pet_part)

    both = lax.all_to_all(parts, ("x", "c"), split_axis=0, concat_axis=0, tiled=True)
    half = lax.axis_index("zh").astype(jnp.int32).reshape(1)
    mr_own, mr_other, pet_own, pet_other = call(
        sum_kernel,
        (sds((2 * ZS, ROW), f32), sds((2 * ZS, ROW), f32), sds((ZS, ROW), f32), sds((ZS, ROW), f32)),
        [SMEM, VMEM], [], 10**6, 10**6, "sums",
    )(half, both)
    places = [(zh, p, j) for zh in range(2) for p in range(8) for j in range(16)]
    mr_a = lax.ppermute(
        mr_own, GRP + GZ, [((zh * 8 + p) * 16 + j, j * 16 + zh * 8 + p) for zh, p, j in places]
    )
    mr_b = lax.ppermute(
        mr_other, GRP + GZ, [((zh * 8 + p) * 16 + j, j * 16 + (1 - zh) * 8 + p) for zh, p, j in places]
    )
    pet_got = lax.ppermute(pet_other, "zh", [(0, 1), (1, 0)])
    return call(
        final_kernel, (sds((ZS, 2, NY), f32), sds((ZS, 2, 2 * NY), f32)), [VMEM] * 6, [],
        10**5, 10**6, "final",
    )(mr_a, mr_b, pet_own, pet_got, couple_pet, couple_mr)


def solution(mesh):
    fine = Mesh(mesh.devices.reshape(2, 4, 2, 4, 4), ("zh", "x", "c", "zl", "y"))
    placed = (
        P(GZ, None, None),
        P(GZ, None, None),
        P(GRP, GZ, None, None),
        P(GRP, None, GZ, None),
        P(),
        P(GRP + GZ, None, None),
        P(GRP + GZ),
        P(GRP + GZ),
        P(GRP, None),
        P(GRP, None),
        P(GRP),
    )
    return jax.shard_map(
        on_device,
        mesh=fine,
        in_specs=placed,
        out_specs=(P(GZ, GRP, None), P(GZ, GRP, None)),
        check_vma=False,
    )
```

```python
import math

import jax
import jax.numpy as jnp
import numpy as np
from jax import lax
from jax.experimental import pallas as pl
from jax.experimental.pallas import tpu as pltpu
from jax.sharding import Mesh, PartitionSpec as P

coupling_weight = 0.1
mag_smooth = 0.3
eta_smooth = 0.3

ZS, NX, NY, NZ = 8, 32, 480, 128
HALF = 512
ROW = 2 * HALF
CHUNK = 152
GRP = ("zh", "x", "c")
GZ = ("zl", "y")
f32, bf16 = jnp.float32, jnp.bfloat16

SMEM = pl.BlockSpec(memory_space=pltpu.SMEM)
VMEM = pl.BlockSpec(memory_space=pltpu.VMEM)
ANY = pl.BlockSpec(memory_space=pl.ANY)


def dft_parts(length):
    indices = np.arange(length)
    angles = (indices[:, None] * indices[None, :] % length) * (2.0 * math.pi / length)
    scaling = 1.0 / math.sqrt(length)
    return np.cos(angles) * scaling, -np.sin(angles) * scaling


def y_table():
    real_part, imag_part = dft_parts(NY)
    table = np.zeros((2, HALF, 2, HALF), np.float64)
    table[0, :NY, 0, :NY] = real_part
    table[0, :NY, 1, :NY] = imag_part
    table[1, :NY, 0, :NY] = -imag_part
    table[1, :NY, 1, :NY] = real_part
    return jnp.asarray(table.reshape(ROW, ROW).astype(jnp.bfloat16))


def z_table():
    real_part, imag_part = dft_parts(NZ)
    table = np.block([[real_part, -imag_part], [imag_part, real_part]])
    return jnp.asarray(table.astype(jnp.bfloat16))


def call(kernel, out_shape, in_specs, scratch, flops, moved, name, out_spec=VMEM, grant=40):
    return pl.pallas_call(
        kernel,
        out_shape=out_shape,
        in_specs=in_specs,
        out_specs=jax.tree.map(lambda _: out_spec, out_shape),
        scratch_shapes=scratch,
        compiler_params=pltpu.CompilerParams(vmem_limit_bytes=grant * 1024 * 1024),
        cost_estimate=pl.CostEstimate(flops=flops, bytes_accessed=moved, transcendentals=0),
        name=name,
    )


def order_tables():
    tables = []
    for count in (2 * ZS, ZS):
        rows = np.arange(NX * count)
        place, q = rows // count, rows % count
        table = np.zeros((NX * count, NX * count), np.float32)
        table[rows, q * NX + 2 * (place % 16) + place // 16] = 1.0
        tables.append(jnp.asarray(table.astype(jnp.bfloat16)))
    return tables


def pack_kernel(core_ref, sens_hbm, mr_hbm, order_hbm, short_hbm, out_hbm, sens_ref, mr_ref, order_ref,
                short_ref, rows_ref, mr_rows, out_ref, sems, out_sems):
    copies = []
    for n in range(4):
        part = pl.ds(64 * n, 64)
        copies.append(pltpu.make_async_copy(mr_hbm.at[part], mr_ref.at[part], sems.at[n]))
    for n in range(4):
        part = pl.ds(128 * n, 128)
        copies.append(pltpu.make_async_copy(sens_hbm.at[part], sens_ref.at[part], sems.at[4 + n]))
    copies.append(pltpu.make_async_copy(order_hbm, order_ref, sems.at[8]))
    copies.append(pltpu.make_async_copy(short_hbm, short_ref, sems.at[9]))
    for copy in copies:
        copy.start()
    imag = core_ref[0] == 1
    rows_ref[256:, HALF + NY :] = jnp.zeros((256, HALF - NY), bf16)
    for n in range(4):
        copies[n].wait()
        part = pl.ds(64 * n, 64)
        values = jnp.where(imag, mr_ref[part, NY:], mr_ref[part, :NY]).astype(bf16)
        mr_rows[part, :] = values[:, :384]
        rows_ref[part, NY:HALF] = values[:, 384:416]
        rows_ref[pl.ds(256 + 64 * n, 64), NY:HALF] = values[:, 416:448]
        rows_ref[part, HALF + NY :] = values[:, 448:]
    for n in range(4):
        copies[4 + n].wait()
        part = pl.ds(128 * n, 128)
        rows_ref[part, :NY] = sens_ref[part, :NY]
        rows_ref[part, HALF : HALF + NY] = sens_ref[part, NY:]
    copies[8].wait()
    copies[9].wait()
    out_copies = []

    def send(rows):
        place = (slice(None), rows)
        copy = pltpu.make_async_copy(out_ref.at[place], out_hbm.at[place], out_sems.at[len(out_copies)])
        copy.start()
        out_copies.append(copy)

    moved = jnp.dot(short_ref[...], mr_rows[...], preferred_element_type=f32)
    blocks = [moved[:, 128 * b : 128 * (b + 1)].reshape(NX, ZS, 128) for b in range(3)]
    out_ref[:, 128:, :] = jnp.concatenate(blocks, 1).astype(bf16)
    for n in range(4):
        moved = jnp.dot(order_ref[...], rows_ref[:, 256 * n : 256 * (n + 1)], preferred_element_type=f32)
        for b in range(2):
            first = 16 * (2 * n + b)
            block = moved[:, 128 * b : 128 * (b + 1)].astype(bf16)
            out_ref[:, first : first + 16, :] = block.reshape(NX, 16, 128)
        send(pl.ds(32 * n, 32))
    send(pl.ds(128, CHUNK - 128))
    for copy in out_copies:
        copy.wait()


def prepare_kernel(core_ref, data_ref, mask_ref, own_out, other_out):
    pad = jnp.zeros((HALF - NY, NZ), f32)

    def turned(values):
        return jnp.concatenate([values.astype(f32), pad], 0).T.astype(bf16)

    for k in range(2):
        for place, out in ((core_ref[0], own_out), (1 - core_ref[0], other_out)):
            for part in range(2):
                values = data_ref[k, place, part * NY : (part + 1) * NY, :]
                out[k, part * NZ : (part + 1) * NZ, :] = turned(values)
    own_out[2, :NZ, :] = turned(mask_ref[...])
    own_out[2, NZ:, :] = jnp.zeros((NZ, HALF), bf16)


def project_kernel(
    info_ref, col_ref, block_ref, xs_ref, pet_ref, mr_ref, tiles_ref,
    pay_ref, win_ref, low_ref, high_ref, picked,
):
    for t in range(16):
        picked[pl.ds(t, 1), :] = pet_ref[pl.ds(col_ref[t], 1), :]
    rows = picked[...].astype(bf16)
    pay_ref[:16, :] = jnp.zeros((16, 128), f32)
    for t in range(16):
        product = jnp.dot(rows, tiles_ref[t], preferred_element_type=f32)
        place = pl.ds(block_ref[t], 1)
        pay_ref[place, :] = pay_ref[place, :] + product[t : t + 1, :]
    win_ref[...] = jnp.zeros((12, ZS, HALF), f32)
    for r in range(4):
        for z in range(ZS):
            place = pl.ds(xs_ref[r] + z * NX, 1)
            win_ref[r, z : z + 1, :NY] = pet_ref[place, :]
            win_ref[4 + r, z : z + 1, :NY] = mr_ref[place, :NY]
            win_ref[8 + r, z : z + 1, :NY] = mr_ref[place, NY:]
    for b in range(4):
        for r in range(12):
            row = pl.ds(12 * b + r, 1)
            low_ref[row, :] = win_ref[r, 0:1, 128 * b : 128 * (b + 1)]
            high_ref[row, :] = win_ref[r, ZS - 1 : ZS, 128 * b : 128 * (b + 1)]
    pay_ref[16:, :] = jnp.where(info_ref[2] == 1, low_ref[...], high_ref[...])


def ratio_rows(block_ref, view_ref, pay_ref, got_ref, measured_ref, background_ref, ratio, gathered):
    for j in range(16):
        counts = measured_ref[pl.ds(view_ref[j], 1), :]
        back = background_ref[pl.ds(view_ref[j], 1), :]
        projection = (pay_ref[j : j + 1, :] + got_ref[j : j + 1, :]) / NY
        ratio[j : j + 1, :] = 1.0 - counts / (projection + back)
    for t in range(16):
        gathered[t : t + 1, :] = ratio[pl.ds(block_ref[t], 1), :]
    return gathered[...].astype(bf16)


def backproject(col_ref, rows, tiles_ref, acc, out_ref):
    acc[...] = jnp.zeros((4, ZS * NX, 128), f32)
    for t in range(16):
        spread = lax.dot_general(
            rows, tiles_ref[t], (((1,), (1,)), ((), ())), preferred_element_type=f32
        )
        place = pl.ds(col_ref[t], 1)
        for b in range(4):
            block = spread[t : t + 1, 128 * b : min(128 * (b + 1), NY)]
            lanes = slice(0, block.shape[1])
            acc[b, place, lanes] = acc[b, place, lanes] + block
    for p in range(16):
        rows_out = slice((2 + p // 8) * ZS, (3 + p // 8) * ZS)
        for k in range(2):
            for b in range(4):
                block = acc[b, pl.ds(2 * p + k, ZS, stride=NX), :] / NY
                first = k * HALF + 128 * b
                out_ref[p % 8, rows_out, first : first + 128] = block.astype(bf16)


def coupling_kernel(
    info_ref, win_ref, got_a, got_b, got_c, got_d, pet_out, mr_out, planes, mags, moved
):
    z_start, x_first = info_ref[0], info_ref[1]
    edges = []
    for which in (info_ref[6], info_ref[7]):
        edge = got_d[16:, :]
        for step, got in enumerate((got_a, got_b, got_c)):
            edge = jnp.where(which == step, got[16:, :], edge)
        edges.append(edge)
    planes[...] = jnp.zeros((12, 24, HALF), f32)
    for r in range(12):
        planes[r, 1 : ZS + 1, :] = win_ref[r]
        for b in range(4):
            lanes = slice(128 * b, 128 * (b + 1))
            planes[r, 0:1, lanes] = edges[0][12 * b + r : 12 * b + r + 1, :]
            planes[r, ZS + 1 : ZS + 2, lanes] = edges[1][12 * b + r : 12 * b + r + 1, :]
    for r in range(4):
        mags[r] = jnp.sqrt(planes[4 + r] ** 2 + planes[8 + r] ** 2 + mag_smooth**2)
    shape = (16, HALF)
    level = z_start - 1 + lax.broadcasted_iota(jnp.int32, shape, 0)
    lane = lax.broadcasted_iota(jnp.int32, shape, 1)
    step_z = level < NZ - 1
    step_y = lane < NY - 1
    term_z = (level >= 0) & (lane < NY)

    def differences(ref, r, step_x):
        here = ref[r, 0:16, :]
        along_z = jnp.where(step_z, ref[r, 1:17, :] - here, 0.0)
        along_x = jnp.where(step_x, ref[r + 1, 0:16, :] - here, 0.0)
        along_y = jnp.where(step_y, pltpu.roll(here, HALF - 1, 1) - here, 0.0)
        return along_z, along_x, along_y

    grads = []
    for r in range(3):
        place = x_first - 1 + r
        step_x = place < NX - 1
        a = differences(planes, r, step_x)
        b = differences(mags, r, step_x)
        a_sq = a[0] ** 2 + a[1] ** 2 + a[2] ** 2
        b_sq = b[0] ** 2 + b[1] ** 2 + b[2] ** 2
        cross = a[0] * b[0] + a[1] * b[1] + a[2] * b[2]
        weight = lax.rsqrt(eta_smooth**2 + a_sq * b_sq - cross * cross)
        weight = jnp.where(term_z & (place >= 0), weight, 0.0)
        grads.append(
            (
                [(p * b_sq - q * cross) * weight for p, q in zip(a, b)],
                [(q * a_sq - p * cross) * weight for p, q in zip(a, b)],
            )
        )

    for k in range(2):
        found = []
        for which in range(2):
            here, before = grads[k + 1][which], grads[k][which]
            total = before[1] - here[0] - here[1] - here[2]
            total = total + pltpu.roll(here[0], 1, 0) + pltpu.roll(here[2], 1, 1)
            found.append(coupling_weight * total)
        moved[0] = found[0]
        scaled = found[1] / mags[k + 1, 0:16, :]
        moved[1] = scaled * planes[5 + k, 0:16, :]
        moved[2] = scaled * planes[9 + k, 0:16, :]
        pet_out[k] = moved[0, 1 : ZS + 1, :]
        mr_out[k, :, :HALF] = moved[1, 1 : ZS + 1, :]
        mr_out[k, :, HALF:] = moved[2, 1 : ZS + 1, :]


def coil_kernel(core_ref, col_ref, block_ref, view_ref, recv_hbm, ytab_hbm, ztab_hbm, data_own_hbm,
                data_got_hbm, tiles_hbm, pay_hbm, got_hbm, measured_hbm, background_hbm,
                out_hbm, recv_ref, ytab_ref, ztab_ref, data_ref, mask_ref, tiles_ref, bins_ref, counts_ref,
                ratio, gathered, acc, sens, images, kyrows, out_ref, sems, out_sems):
    copies = []

    def fetch(source, target):
        copies.append(pltpu.make_async_copy(source, target, sems.at[len(copies)]))
        copies[-1].start()
        return copies[-1]

    small = [
        fetch(pay_hbm, bins_ref.at[0]), fetch(got_hbm, bins_ref.at[1]),
        fetch(measured_hbm, counts_ref.at[0]), fetch(background_hbm, counts_ref.at[1]),
    ]
    received = [fetch(recv_hbm.at[pl.ds(8 * n, 8)], recv_ref.at[pl.ds(8 * n, 8)]) for n in range(4)]
    tables = [
        fetch(ytab_hbm.at[pl.ds(256 * n, 256)], ytab_ref.at[pl.ds(256 * n, 256)]) for n in range(4)
    ]
    others = [
        fetch(ztab_hbm, ztab_ref),
        fetch(data_own_hbm.at[pl.ds(0, 2)], data_ref.at[core_ref[0]]),
        fetch(data_got_hbm, data_ref.at[1 - core_ref[0]]),
        fetch(data_own_hbm.at[2], mask_ref),
    ]
    tiles = [fetch(tiles_hbm.at[pl.ds(4 * n, 4)], tiles_ref.at[pl.ds(4 * n, 4)]) for n in range(4)]
    for copy in small:
        copy.wait()
    ratio_now = ratio_rows(
        block_ref, view_ref, bins_ref.at[0], bins_ref.at[1], counts_ref.at[0], counts_ref.at[1], ratio, gathered
    )
    for copy in received:
        copy.wait()

    def block(c, b):
        return recv_ref[16 * c : 16 * (c + 1), 16 * b : 16 * (b + 1), :].astype(f32)

    lane = lax.broadcasted_iota(jnp.int32, (NZ, 128), 1)

    def image_part(c):
        tail = recv_ref[16 * c : 16 * (c + 1), 128:, :].astype(f32)
        parts = [tail[:, ZS * b : ZS * (b + 1)].reshape(NZ, 128) for b in range(3)]
        real, imag = block(c, 3), block(c, 7)
        first = pltpu.roll(real[:, :ZS].reshape(NZ, 128), 32, 1)
        second = pltpu.roll(real[:, ZS:].reshape(NZ, 128), 64, 1)
        third = pltpu.roll(imag[:, :ZS].reshape(NZ, 128), 96, 1)
        last = jnp.where(lane < 32, first, jnp.where(lane < 64, second, third))
        return jnp.concatenate(parts + [jnp.where(lane < 96, last, 0.0)], -1)

    mr_re, mr_im = image_part(0), image_part(1)
    for c in range(2):
        for b in range(4):
            real, imag = block(c, b), block(c, 4 + b)
            lanes = slice(128 * b, 128 * (b + 1))
            lanes_im = slice(HALF + 128 * b, HALF + 128 * (b + 1))
            for k in range(2):
                rows = pl.ds((2 * c + k) * NZ, NZ)
                s_re = real[:, k * ZS : (k + 1) * ZS].reshape(NZ, 128)
                s_im = imag[:, k * ZS : (k + 1) * ZS].reshape(NZ, 128)
                sens[rows, lanes] = s_re
                sens[rows, lanes_im] = s_im
                images[rows, lanes] = (s_re * mr_re[:, lanes] - s_im * mr_im[:, lanes]).astype(bf16)
                images[rows, lanes_im] = (s_re * mr_im[:, lanes] + s_im * mr_re[:, lanes]).astype(bf16)
    for copy in tables:
        copy.wait()
    kyrows[...] = jnp.dot(images[...], ytab_ref[...], preferred_element_type=f32).astype(bf16)
    for copy in others:
        copy.wait()
    mask = mask_ref[:NZ, :].astype(f32)
    ztab = ztab_ref[...]
    for q in range(4):
        rows = pl.ds(q * NZ, NZ)
        volume = jnp.concatenate([kyrows[rows, :HALF], kyrows[rows, HALF:]], 0)
        kspace = jnp.dot(ztab, volume, preferred_element_type=f32)
        data = data_ref[q // 2, q % 2].astype(f32)
        misfit = jnp.concatenate(
            [mask * (kspace[:NZ] - data[:NZ]), mask * (data[NZ:] - kspace[NZ:])], 0
        ).astype(bf16)
        back = jnp.dot(ztab, misfit, preferred_element_type=f32).astype(bf16)
        images[rows, :HALF] = back[:NZ]
        images[rows, HALF:] = back[NZ:]
    for copy in tiles:
        copy.wait()
    backproject(col_ref, ratio_now, tiles_ref, acc, out_ref)
    for b in range(4):
        lanes = slice(128 * b, 128 * (b + 1))
        lanes_im = slice(HALF + 128 * b, HALF + 128 * (b + 1))
        table = jnp.concatenate([ytab_ref[:, lanes], ytab_ref[:, lanes_im]], 1)
        image = jnp.dot(images[...], table, preferred_element_type=f32)
        total_re = jnp.zeros((NZ, 128), f32)
        total_im = jnp.zeros((NZ, 128), f32)
        for q in range(4):
            rows = slice(q * NZ, (q + 1) * NZ)
            s_re, s_im = sens[rows, lanes], sens[rows, lanes_im]
            i_re, i_im = image[rows, :128], image[rows, 128:]
            total_re = total_re + (s_re * i_re - s_im * i_im)
            total_im = total_im - (s_re * i_im + s_im * i_re)
        for total, place in ((total_re, lanes), (total_im, lanes_im)):
            slabs = total.reshape(2, 8, ZS, 128)
            out_ref[:, : 2 * ZS, place] = jnp.concatenate([slabs[0], slabs[1]], 1).astype(bf16)
    out_copies = []
    for n in range(2):
        part = pl.ds(4 * n, 4)
        out_copies.append(pltpu.make_async_copy(out_ref.at[part], out_hbm.at[part], out_sems.at[n]))
        out_copies[-1].start()
    for copy in out_copies:
        copy.wait()


def sum_kernel(half_ref, recv_ref, mr_own, mr_other, pet_own, pet_other):
    upper = half_ref[0] == 1
    pet = jnp.zeros((2 * ZS, ROW), f32)
    for c in range(2):
        mr = jnp.zeros((2 * ZS, ROW), f32)
        for x in range(4):
            block = recv_ref[2 * x + c].astype(f32)
            mr = mr + block[: 2 * ZS]
            pet = pet + block[2 * ZS :]
        rows = pl.ds(c * ZS, ZS)
        mr_own[rows, :] = jnp.where(upper, mr[ZS:], mr[:ZS]).astype(bf16)
        mr_other[rows, :] = jnp.where(upper, mr[:ZS], mr[ZS:]).astype(bf16)
    pet_own[...] = jnp.where(upper, pet[ZS:], pet[:ZS])
    pet_other[...] = jnp.where(upper, pet[:ZS], pet[ZS:]).astype(bf16)


def final_kernel(mr_a, mr_b, pet_a, pet_b, couple_pet_ref, couple_mr_ref, pet_out, mr_out):
    for k in range(2):
        rows = pl.ds(k * ZS, ZS)
        lanes = pl.ds(k * HALF, HALF)
        pet = pet_a[:, lanes] + pet_b[:, lanes].astype(f32) + couple_pet_ref[k]
        mr = mr_a[rows, :].astype(f32) + mr_b[rows, :].astype(f32) + couple_mr_ref[k]
        pet_out[:, k, :] = pet[:, :NY]
        mr_out[:, k, :NY] = mr[:, :NY]
        mr_out[:, k, NY:] = mr[:, HALF : HALF + NY]


def sds(shape, dtype):
    return jax.ShapeDtypeStruct(shape, dtype)


def on_device(
    pet_image, mr_image, coil_sens, kspace_data, kspace_mask, system_tiles,
    tile_subset_block, tile_col, measured, background, subset_view_blocks,
):
    core = lax.axis_index("c")
    grp = lax.axis_index(GRP)
    gz = lax.axis_index(GZ)
    core_arr = core.astype(jnp.int32).reshape(1)
    pet_rows = pet_image.reshape(ZS * NX, NY)
    mr_rows = mr_image.reshape(ZS * NX, 2 * NY)
    tiles = system_tiles.swapaxes(1, 2)

    sent = call(
        pack_kernel, sds((32, CHUNK, 128), bf16), [SMEM] + [ANY] * 4,
        [pltpu.VMEM((2 * ZS * NX, 2 * NY), bf16), pltpu.VMEM((ZS * NX, 2 * NY), f32),
         pltpu.VMEM((512, 512), bf16), pltpu.VMEM((256, 256), bf16), pltpu.VMEM((512, ROW), bf16),
         pltpu.VMEM((256, 384), bf16), pltpu.VMEM((32, CHUNK, 128), bf16),
         pltpu.SemaphoreType.DMA((10,)), pltpu.SemaphoreType.DMA((5,))],
        10**6, 4 * 10**6, "pack", ANY, 60,
    )(core_arr, coil_sens.reshape(2 * ZS * NX, 2 * NY), mr_rows, *order_tables())
    sent, tile_col = lax.optimization_barrier((sent, tile_col))
    recv = lax.all_to_all(sent, ("c",) + GZ, split_axis=0, concat_axis=0, tiled=True)

    xs = jnp.clip(2 * grp - 1 + jnp.arange(4, dtype=jnp.int32), 0, NX - 1)
    bits = [(gz >> t) & 1 for t in range(4)]
    ones = [gz & 1, (gz & 3) == 3, (gz & 7) == 7]
    zeros = [(gz & 1) == 0, (gz & 3) == 0, (gz & 7) == 0]
    after = sum(jnp.asarray(v).astype(jnp.int32) for v in ones)
    before = sum(jnp.asarray(v).astype(jnp.int32) for v in zeros)
    info = jnp.stack([gz * ZS, 2 * grp] + bits + [before, after]).astype(jnp.int32)
    pay, win, low, high = call(
        project_kernel,
        (sds((64, 128), f32), sds((12, ZS, HALF), f32), sds((48, 128), f32), sds((48, 128), f32)),
        [SMEM] * 4 + [VMEM] * 3, [pltpu.VMEM((16, NY), f32)],
        10**7, 4 * 10**6, "project", VMEM, 8,
    )(info, tile_col, tile_subset_block, xs, pet_rows, mr_rows, tiles)
    got = []
    for step in range(4):
        got.append(lax.ppermute(pay, GZ, [(i, i ^ (2 ** (step + 1) - 1)) for i in range(16)]))
        if step == 0:
            kspace_data, got[0] = lax.optimization_barrier((kspace_data, got[0]))
        if step < 3:
            edge = jnp.where(bits[step + 1] == 1, low, high)
            pay = jnp.concatenate([pay[:16] + got[step][:16], edge], 0)
    data_own, data_out = call(
        prepare_kernel, (sds((3, 2 * NZ, HALF), bf16), sds((2, 2 * NZ, HALF), bf16)),
        [SMEM, VMEM, VMEM], [], 10**6, 3 * 10**6, "prepare", VMEM, 8,
    )(core_arr, kspace_data.transpose(0, 2, 3, 1), kspace_mask.T)
    data_got = lax.ppermute(data_out, "c", [(0, 1), (1, 0)])
    couple_pet, couple_mr = call(
        coupling_kernel, (sds((2, ZS, HALF), f32), sds((2, ZS, ROW), f32)),
        [SMEM] + [VMEM] * 5,
        [pltpu.VMEM((12, 24, HALF), f32), pltpu.VMEM((4, 24, HALF), f32),
         pltpu.VMEM((3, 16, HALF), f32)],
        10**6, 10**6, "coupling", VMEM, 8,
    )(info, win, *got)

    parts = call(
        coil_kernel, sds((8, 4 * ZS, ROW), bf16), [SMEM] * 4 + [ANY] * 10,
        [pltpu.VMEM((32, CHUNK, 128), bf16), pltpu.VMEM((ROW, ROW), bf16),
         pltpu.VMEM((2 * NZ, 2 * NZ), bf16), pltpu.VMEM((2, 2, 2 * NZ, HALF), bf16),
         pltpu.VMEM((2 * NZ, HALF), bf16), pltpu.VMEM((16, NY, 128), bf16),
         pltpu.VMEM((2, 64, 128), f32), pltpu.VMEM((2, 64, 128), f32),
         pltpu.VMEM((16, 128), f32), pltpu.VMEM((16, 128), f32), pltpu.VMEM((4, ZS * NX, 128), f32),
         pltpu.VMEM((4 * NZ, ROW), f32), pltpu.VMEM((4 * NZ, ROW), bf16),
         pltpu.VMEM((4 * NZ, ROW), bf16), pltpu.VMEM((8, 4 * ZS, ROW), bf16),
         pltpu.SemaphoreType.DMA((20,)), pltpu.SemaphoreType.DMA((2,))],
        5 * 10**9, 6 * 10**6, "coils", ANY, 61,
    )(core_arr, tile_col, tile_subset_block, subset_view_blocks, recv, y_table(), z_table(), data_own,
      data_got, tiles, pay, got[3], measured, background)

    both = lax.all_to_all(parts, ("x", "c"), split_axis=0, concat_axis=0, tiled=True)
    half = lax.axis_index("zh").astype(jnp.int32).reshape(1)
    mr_own, mr_other, pet_own, pet_other = call(
        sum_kernel,
        (sds((2 * ZS, ROW), bf16), sds((2 * ZS, ROW), bf16), sds((ZS, ROW), f32), sds((ZS, ROW), bf16)),
        [SMEM, VMEM], [], 10**6, 10**6, "sums",
    )(half, both)
    places = [(zh, p, j) for zh in range(2) for p in range(8) for j in range(16)]
    mr_a = lax.ppermute(
        mr_own, GRP + GZ, [((zh * 8 + p) * 16 + j, j * 16 + zh * 8 + p) for zh, p, j in places]
    )
    mr_b = lax.ppermute(
        mr_other, GRP + GZ, [((zh * 8 + p) * 16 + j, j * 16 + (1 - zh) * 8 + p) for zh, p, j in places]
    )
    pet_got = lax.ppermute(pet_other, "zh", [(0, 1), (1, 0)])
    return call(
        final_kernel, (sds((ZS, 2, NY), f32), sds((ZS, 2, 2 * NY), f32)), [VMEM] * 6, [],
        10**5, 10**6, "final",
    )(mr_a, mr_b, pet_own, pet_got, couple_pet, couple_mr)


def solution(mesh):
    fine = Mesh(mesh.devices.reshape(2, 4, 2, 4, 4), ("zh", "x", "c", "zl", "y"))
    placed = (
        P(GZ, None, None),
        P(GZ, None, None),
        P(GRP, GZ, None, None),
        P(GRP, None, GZ, None),
        P(),
        P(GRP + GZ, None, None),
        P(GRP + GZ),
        P(GRP + GZ),
        P(GRP, None),
        P(GRP, None),
        P(GRP),
    )
    return jax.shard_map(
        on_device,
        mesh=fine,
        in_specs=placed,
        out_specs=(P(GZ, GRP, None), P(GZ, GRP, None)),
        check_vma=False,
    )
```

```python
import math

import jax
import jax.numpy as jnp
import numpy as np
from jax import lax
from jax.experimental import pallas as pl
from jax.experimental.pallas import tpu as pltpu
from jax.sharding import Mesh, PartitionSpec as P

coupling_weight = 0.1
mag_smooth = 0.3
eta_smooth = 0.3

ZS, NX, NY, NZ = 8, 32, 480, 128
HALF = 512
ROW = 2 * HALF
CHUNK = 152
GRP = ("zh", "x", "c")
GZ = ("zl", "y")
f32, bf16 = jnp.float32, jnp.bfloat16

SMEM = pl.BlockSpec(memory_space=pltpu.SMEM)
VMEM = pl.BlockSpec(memory_space=pltpu.VMEM)
ANY = pl.BlockSpec(memory_space=pl.ANY)


def dft_parts(length):
    indices = np.arange(length)
    angles = (indices[:, None] * indices[None, :] % length) * (2.0 * math.pi / length)
    scaling = 1.0 / math.sqrt(length)
    return np.cos(angles) * scaling, -np.sin(angles) * scaling


def y_table():
    real_part, imag_part = dft_parts(NY)
    table = np.zeros((2, HALF, 2, HALF), np.float64)
    table[0, :NY, 0, :NY] = real_part
    table[0, :NY, 1, :NY] = imag_part
    table[1, :NY, 0, :NY] = -imag_part
    table[1, :NY, 1, :NY] = real_part
    return jnp.asarray(table.reshape(ROW, ROW).astype(jnp.bfloat16))


def arrived(slab):
    return slab % 4 * 4 + slab // 4


def z_tables():
    real_part, imag_part = dft_parts(NZ)
    table = np.block([[real_part, -imag_part], [imag_part, real_part]])
    place = np.arange(NZ)
    order = arrived(place // ZS) * ZS + place % ZS
    order = np.concatenate([order, NZ + order])
    return jnp.asarray(np.stack([table[:, order], table[order]]).astype(jnp.bfloat16))


def call(kernel, out_shape, in_specs, scratch, flops, moved, name, out_spec=VMEM, grant=40):
    return pl.pallas_call(
        kernel,
        out_shape=out_shape,
        in_specs=in_specs,
        out_specs=jax.tree.map(lambda _: out_spec, out_shape),
        scratch_shapes=scratch,
        compiler_params=pltpu.CompilerParams(vmem_limit_bytes=grant * 1024 * 1024),
        cost_estimate=pl.CostEstimate(flops=flops, bytes_accessed=moved, transcendentals=0),
        name=name,
    )


def pack_kernel(core_ref, sens_hbm, mr_hbm, out_hbm, sens_ref, mr_ref, order_ref, short_ref, rows_ref,
                mr_rows, out_ref, sems, out_sems):
    copies = []
    for n in range(4):
        part = pl.ds(128 * n, 128)
        copies.append(pltpu.make_async_copy(sens_hbm.at[part], sens_ref.at[part], sems.at[n]))
    for n in range(4):
        part = pl.ds(64 * n, 64)
        copies.append(pltpu.make_async_copy(mr_hbm.at[part], mr_ref.at[part], sems.at[4 + n]))
    for copy in copies:
        copy.start()
    for count, ref in ((2 * ZS, order_ref), (ZS, short_ref)):
        size = NX * count
        row = lax.broadcasted_iota(jnp.int32, (size, size), 0)
        col = lax.broadcasted_iota(jnp.int32, (size, size), 1)
        place, q = row // count, row % count
        source = q * NX + 2 * (place % 4 * 4 + place % 16 // 4) + place // 16
        ref[...] = jnp.where(col == source, 1.0, 0.0).astype(bf16)
    imag = core_ref[0] == 1
    rows_ref[256:, HALF + NY :] = jnp.zeros((256, HALF - NY), bf16)
    out_copies = []

    def send(rows):
        place = (slice(None), rows)
        copy = pltpu.make_async_copy(out_ref.at[place], out_hbm.at[place], out_sems.at[len(out_copies)])
        copy.start()
        out_copies.append(copy)

    for n in range(4):
        copies[n].wait()
        part = pl.ds(128 * n, 128)
        rows_ref[part, :NY] = sens_ref[part, :NY]
        rows_ref[part, HALF : HALF + NY] = sens_ref[part, NY:]
    for n in range(4):
        copies[4 + n].wait()
        part = pl.ds(64 * n, 64)
        values = jnp.where(imag, mr_ref[part, NY:], mr_ref[part, :NY]).astype(bf16)
        mr_rows[part, :] = values[:, :384]
        rows_ref[part, NY:HALF] = values[:, 384:416]
        rows_ref[pl.ds(256 + 64 * n, 64), NY:HALF] = values[:, 416:448]
        rows_ref[part, HALF + NY :] = values[:, 448:]
    for n in range(4):
        moved = jnp.dot(order_ref[...], rows_ref[:, 256 * n : 256 * (n + 1)], preferred_element_type=f32)
        for b in range(2):
            first = 16 * (2 * n + b)
            block = moved[:, 128 * b : 128 * (b + 1)].astype(bf16)
            out_ref[:, first : first + 16, :] = block.reshape(NX, 16, 128)
        send(pl.ds(32 * n, 32))
    moved = jnp.dot(short_ref[...], mr_rows[...], preferred_element_type=f32)
    blocks = [moved[:, 128 * b : 128 * (b + 1)].reshape(NX, ZS, 128) for b in range(3)]
    out_ref[:, 128:, :] = jnp.concatenate(blocks, 1).astype(bf16)
    send(pl.ds(128, CHUNK - 128))
    for copy in out_copies:
        copy.wait()


def prepare_kernel(core_ref, data_ref, mask_ref, own_out, other_out):
    pad = jnp.zeros((HALF - NY, NZ), f32)

    def turned(values):
        return jnp.concatenate([values.astype(f32), pad], 0).T.astype(bf16)

    for k in range(2):
        for place, out in ((core_ref[0], own_out), (1 - core_ref[0], other_out)):
            for part in range(2):
                values = data_ref[k, place, part * NY : (part + 1) * NY, :]
                out[k, part * NZ : (part + 1) * NZ, :] = turned(values)
    own_out[2, :NZ, :] = turned(mask_ref[...])
    own_out[2, NZ:, :] = jnp.zeros((NZ, HALF), bf16)


def project_kernel(
    info_ref, col_ref, block_ref, xs_ref, pet_ref, mr_ref, tiles_ref,
    pay_ref, win_ref, low_ref, high_ref, picked,
):
    for t in range(16):
        picked[pl.ds(t, 1), :] = pet_ref[pl.ds(col_ref[t], 1), :]
    rows = picked[...].astype(bf16)
    pay_ref[:16, :] = jnp.zeros((16, 128), f32)
    for t in range(16):
        product = jnp.dot(rows, tiles_ref[t], preferred_element_type=f32)
        place = pl.ds(block_ref[t], 1)
        pay_ref[place, :] = pay_ref[place, :] + product[t : t + 1, :]
    win_ref[...] = jnp.zeros((12, ZS, HALF), f32)
    for r in range(4):
        for z in range(ZS):
            place = pl.ds(xs_ref[r] + z * NX, 1)
            win_ref[r, z : z + 1, :NY] = pet_ref[place, :]
            win_ref[4 + r, z : z + 1, :NY] = mr_ref[place, :NY]
            win_ref[8 + r, z : z + 1, :NY] = mr_ref[place, NY:]
    for b in range(4):
        for r in range(12):
            row = pl.ds(12 * b + r, 1)
            low_ref[row, :] = win_ref[r, 0:1, 128 * b : 128 * (b + 1)]
            high_ref[row, :] = win_ref[r, ZS - 1 : ZS, 128 * b : 128 * (b + 1)]
    pay_ref[16:, :] = jnp.where(info_ref[2] == 1, low_ref[...], high_ref[...])


def ratio_rows(block_ref, view_ref, pay_ref, got_ref, measured_ref, background_ref, ratio, gathered):
    for j in range(16):
        counts = measured_ref[pl.ds(view_ref[j], 1), :]
        back = background_ref[pl.ds(view_ref[j], 1), :]
        projection = (pay_ref[j : j + 1, :] + got_ref[j : j + 1, :]) / NY
        ratio[j : j + 1, :] = 1.0 - counts / (projection + back)
    for t in range(16):
        gathered[t : t + 1, :] = ratio[pl.ds(block_ref[t], 1), :]
    return gathered[...].astype(bf16)


def backproject(col_ref, rows, tiles_ref, acc, out_ref):
    acc[...] = jnp.zeros((4, ZS * NX, 128), f32)
    for t in range(16):
        spread = lax.dot_general(
            rows, tiles_ref[t], (((1,), (1,)), ((), ())), preferred_element_type=f32
        )
        place = pl.ds(col_ref[t], 1)
        for b in range(4):
            block = spread[t : t + 1, 128 * b : min(128 * (b + 1), NY)]
            lanes = slice(0, block.shape[1])
            acc[b, place, lanes] = acc[b, place, lanes] + block
    for p in range(16):
        rows_out = slice((2 + p // 8) * ZS, (3 + p // 8) * ZS)
        for k in range(2):
            for b in range(4):
                block = acc[b, pl.ds(2 * p + k, ZS, stride=NX), :] / NY
                first = k * HALF + 128 * b
                out_ref[p % 8, rows_out, first : first + 128] = block.astype(bf16)


def coupling_kernel(
    info_ref, win_ref, got_a, got_b, got_c, got_d, pet_out, mr_out, planes, mags, moved
):
    z_start, x_first = info_ref[0], info_ref[1]
    edges = []
    for which in (info_ref[6], info_ref[7]):
        edge = got_d[16:, :]
        for step, got in enumerate((got_a, got_b, got_c)):
            edge = jnp.where(which == step, got[16:, :], edge)
        edges.append(edge)
    planes[...] = jnp.zeros((12, 24, HALF), f32)
    for r in range(12):
        planes[r, 1 : ZS + 1, :] = win_ref[r]
        for b in range(4):
            lanes = slice(128 * b, 128 * (b + 1))
            planes[r, 0:1, lanes] = edges[0][12 * b + r : 12 * b + r + 1, :]
            planes[r, ZS + 1 : ZS + 2, lanes] = edges[1][12 * b + r : 12 * b + r + 1, :]
    for r in range(4):
        mags[r] = jnp.sqrt(planes[4 + r] ** 2 + planes[8 + r] ** 2 + mag_smooth**2)
    shape = (16, HALF)
    level = z_start - 1 + lax.broadcasted_iota(jnp.int32, shape, 0)
    lane = lax.broadcasted_iota(jnp.int32, shape, 1)
    step_z = level < NZ - 1
    step_y = lane < NY - 1
    term_z = (level >= 0) & (lane < NY)

    def differences(ref, r, step_x):
        here = ref[r, 0:16, :]
        along_z = jnp.where(step_z, ref[r, 1:17, :] - here, 0.0)
        along_x = jnp.where(step_x, ref[r + 1, 0:16, :] - here, 0.0)
        along_y = jnp.where(step_y, pltpu.roll(here, HALF - 1, 1) - here, 0.0)
        return along_z, along_x, along_y

    grads = []
    for r in range(3):
        place = x_first - 1 + r
        step_x = place < NX - 1
        a = differences(planes, r, step_x)
        b = differences(mags, r, step_x)
        a_sq = a[0] ** 2 + a[1] ** 2 + a[2] ** 2
        b_sq = b[0] ** 2 + b[1] ** 2 + b[2] ** 2
        cross = a[0] * b[0] + a[1] * b[1] + a[2] * b[2]
        weight = lax.rsqrt(eta_smooth**2 + a_sq * b_sq - cross * cross)
        weight = jnp.where(term_z & (place >= 0), weight, 0.0)
        grads.append(
            (
                [(p * b_sq - q * cross) * weight for p, q in zip(a, b)],
                [(q * a_sq - p * cross) * weight for p, q in zip(a, b)],
            )
        )

    for k in range(2):
        found = []
        for which in range(2):
            here, before = grads[k + 1][which], grads[k][which]
            total = before[1] - here[0] - here[1] - here[2]
            total = total + pltpu.roll(here[0], 1, 0) + pltpu.roll(here[2], 1, 1)
            found.append(coupling_weight * total)
        moved[0] = found[0]
        scaled = found[1] / mags[k + 1, 0:16, :]
        moved[1] = scaled * planes[5 + k, 0:16, :]
        moved[2] = scaled * planes[9 + k, 0:16, :]
        pet_out[k] = moved[0, 1 : ZS + 1, :]
        mr_out[k, :, :HALF] = moved[1, 1 : ZS + 1, :]
        mr_out[k, :, HALF:] = moved[2, 1 : ZS + 1, :]


def coil_kernel(core_ref, col_ref, block_ref, view_ref, recv_hbm, ytab_hbm, ztab_hbm, data_own_hbm,
                data_got_hbm, tiles_hbm, pay_hbm, got_hbm, measured_hbm, background_hbm,
                out_hbm, recv_ref, ytab_ref, ztab_ref, data_ref, mask_ref, tiles_ref, bins_ref, counts_ref,
                ratio, gathered, acc, sens, images, kyrows, out_ref, sems, out_sems):
    copies = []

    def fetch(source, target):
        copies.append(pltpu.make_async_copy(source, target, sems.at[len(copies)]))
        copies[-1].start()
        return copies[-1]

    small = [
        fetch(pay_hbm, bins_ref.at[0]), fetch(got_hbm, bins_ref.at[1]),
        fetch(measured_hbm, counts_ref.at[0]), fetch(background_hbm, counts_ref.at[1]),
    ]
    received = [fetch(recv_hbm.at[pl.ds(8 * n, 8)], recv_ref.at[pl.ds(8 * n, 8)]) for n in range(4)]
    tables = [
        fetch(ytab_hbm.at[pl.ds(256 * n, 256)], ytab_ref.at[pl.ds(256 * n, 256)]) for n in range(4)
    ]
    others = [
        fetch(ztab_hbm, ztab_ref),
        fetch(data_own_hbm.at[pl.ds(0, 2)], data_ref.at[core_ref[0]]),
        fetch(data_got_hbm, data_ref.at[1 - core_ref[0]]),
        fetch(data_own_hbm.at[2], mask_ref),
    ]
    tiles = [fetch(tiles_hbm.at[pl.ds(4 * n, 4)], tiles_ref.at[pl.ds(4 * n, 4)]) for n in range(4)]
    for copy in small:
        copy.wait()
    ratio_now = ratio_rows(
        block_ref, view_ref, bins_ref.at[0], bins_ref.at[1], counts_ref.at[0], counts_ref.at[1], ratio, gathered
    )
    for copy in received:
        copy.wait()

    def block(c, b):
        return recv_ref[16 * c : 16 * (c + 1), 16 * b : 16 * (b + 1), :].astype(f32)

    lane = lax.broadcasted_iota(jnp.int32, (NZ, 128), 1)

    def image_part(c):
        tail = recv_ref[16 * c : 16 * (c + 1), 128:, :].astype(f32)
        parts = [tail[:, ZS * b : ZS * (b + 1)].reshape(NZ, 128) for b in range(3)]
        real, imag = block(c, 3), block(c, 7)
        first = pltpu.roll(real[:, :ZS].reshape(NZ, 128), 32, 1)
        second = pltpu.roll(real[:, ZS:].reshape(NZ, 128), 64, 1)
        third = pltpu.roll(imag[:, :ZS].reshape(NZ, 128), 96, 1)
        last = jnp.where(lane < 32, first, jnp.where(lane < 64, second, third))
        return jnp.concatenate(parts + [jnp.where(lane < 96, last, 0.0)], -1)

    mr_re, mr_im = image_part(0), image_part(1)
    for c in range(2):
        for b in range(4):
            real, imag = block(c, b), block(c, 4 + b)
            lanes = slice(128 * b, 128 * (b + 1))
            lanes_im = slice(HALF + 128 * b, HALF + 128 * (b + 1))
            for k in range(2):
                rows = pl.ds((2 * c + k) * NZ, NZ)
                s_re = real[:, k * ZS : (k + 1) * ZS].reshape(NZ, 128)
                s_im = imag[:, k * ZS : (k + 1) * ZS].reshape(NZ, 128)
                sens[rows, lanes] = s_re
                sens[rows, lanes_im] = s_im
                images[rows, lanes] = (s_re * mr_re[:, lanes] - s_im * mr_im[:, lanes]).astype(bf16)
                images[rows, lanes_im] = (s_re * mr_im[:, lanes] + s_im * mr_re[:, lanes]).astype(bf16)
    for copy in tables:
        copy.wait()
    kyrows[...] = jnp.dot(images[...], ytab_ref[...], preferred_element_type=f32).astype(bf16)
    for copy in others:
        copy.wait()
    mask = mask_ref[:NZ, :].astype(f32)
    for q in range(4):
        rows = pl.ds(q * NZ, NZ)
        volume = jnp.concatenate([kyrows[rows, :HALF], kyrows[rows, HALF:]], 0)
        kspace = jnp.dot(ztab_ref[0], volume, preferred_element_type=f32)
        data = data_ref[q // 2, q % 2].astype(f32)
        misfit = jnp.concatenate(
            [mask * (kspace[:NZ] - data[:NZ]), mask * (data[NZ:] - kspace[NZ:])], 0
        ).astype(bf16)
        back = jnp.dot(ztab_ref[1], misfit, preferred_element_type=f32).astype(bf16)
        images[rows, :HALF] = back[:NZ]
        images[rows, HALF:] = back[NZ:]
    for copy in tiles:
        copy.wait()
    backproject(col_ref, ratio_now, tiles_ref, acc, out_ref)
    out_copies = []
    for n in (1, 0):
        part = (slice(None), pl.ds(2 * ZS * n, 2 * ZS))
        out_copies.append(pltpu.make_async_copy(out_ref.at[part], out_hbm.at[part], out_sems.at[n]))
    out_copies[0].start()
    for b in range(4):
        lanes = slice(128 * b, 128 * (b + 1))
        lanes_im = slice(HALF + 128 * b, HALF + 128 * (b + 1))
        table = jnp.concatenate([ytab_ref[:, lanes], ytab_ref[:, lanes_im]], 1)
        image = jnp.dot(images[...], table, preferred_element_type=f32)
        total_re = jnp.zeros((NZ, 128), f32)
        total_im = jnp.zeros((NZ, 128), f32)
        for q in range(4):
            rows = slice(q * NZ, (q + 1) * NZ)
            s_re, s_im = sens[rows, lanes], sens[rows, lanes_im]
            i_re, i_im = image[rows, :128], image[rows, 128:]
            total_re = total_re + (s_re * i_re - s_im * i_im)
            total_im = total_im - (s_re * i_im + s_im * i_re)
        for total, place in ((total_re, lanes), (total_im, lanes_im)):
            slabs = total.reshape(16, ZS, 128)
            for p in range(8):
                both = jnp.concatenate([slabs[arrived(p)], slabs[arrived(p + 8)]], 0)
                out_ref[p, : 2 * ZS, place] = both.astype(bf16)
    out_copies[1].start()
    for copy in out_copies:
        copy.wait()


def sum_kernel(half_ref, recv_ref, mr_own, mr_other, pet_own, pet_other):
    upper = half_ref[0] == 1
    pet = jnp.zeros((2 * ZS, ROW), f32)
    for c in range(2):
        mr = jnp.zeros((2 * ZS, ROW), f32)
        for x in range(4):
            block = recv_ref[2 * x + c].astype(f32)
            mr = mr + block[: 2 * ZS]
            pet = pet + block[2 * ZS :]
        rows = pl.ds(c * ZS, ZS)
        mr_own[rows, :] = jnp.where(upper, mr[ZS:], mr[:ZS]).astype(bf16)
        mr_other[rows, :] = jnp.where(upper, mr[:ZS], mr[ZS:]).astype(bf16)
    pet_own[...] = jnp.where(upper, pet[ZS:], pet[:ZS])
    pet_other[...] = jnp.where(upper, pet[:ZS], pet[ZS:]).astype(bf16)


def final_kernel(mr_a, mr_b, pet_a, pet_b, couple_pet_ref, couple_mr_ref, pet_out, mr_out):
    for k in range(2):
        rows = pl.ds(k * ZS, ZS)
        lanes = pl.ds(k * HALF, HALF)
        pet = pet_a[:, lanes] + pet_b[:, lanes].astype(f32) + couple_pet_ref[k]
        mr = mr_a[rows, :].astype(f32) + mr_b[rows, :].astype(f32) + couple_mr_ref[k]
        pet_out[:, k, :] = pet[:, :NY]
        mr_out[:, k, :NY] = mr[:, :NY]
        mr_out[:, k, NY:] = mr[:, HALF : HALF + NY]


def sds(shape, dtype):
    return jax.ShapeDtypeStruct(shape, dtype)


def on_device(
    pet_image, mr_image, coil_sens, kspace_data, kspace_mask, system_tiles,
    tile_subset_block, tile_col, measured, background, subset_view_blocks,
):
    core = lax.axis_index("c")
    grp = lax.axis_index(GRP)
    gz = lax.axis_index(GZ)
    core_arr = core.astype(jnp.int32).reshape(1)
    pet_rows = pet_image.reshape(ZS * NX, NY)
    mr_rows = mr_image.reshape(ZS * NX, 2 * NY)
    tiles = system_tiles.swapaxes(1, 2)

    sent = call(
        pack_kernel, sds((32, CHUNK, 128), bf16), [SMEM] + [ANY] * 2,
        [pltpu.VMEM((2 * ZS * NX, 2 * NY), bf16), pltpu.VMEM((ZS * NX, 2 * NY), f32),
         pltpu.VMEM((512, 512), bf16), pltpu.VMEM((256, 256), bf16), pltpu.VMEM((512, ROW), bf16),
         pltpu.VMEM((256, 384), bf16), pltpu.VMEM((32, CHUNK, 128), bf16),
         pltpu.SemaphoreType.DMA((8,)), pltpu.SemaphoreType.DMA((5,))],
        10**9, 4 * 10**6, "pack", ANY, 60,
    )(core_arr, coil_sens.reshape(2 * ZS * NX, 2 * NY), mr_rows)
    sent, tile_col = lax.optimization_barrier((sent, tile_col))
    recv = lax.all_to_all(sent, ("c", "y", "zl"), split_axis=0, concat_axis=0, tiled=True)

    xs = jnp.clip(2 * grp - 1 + jnp.arange(4, dtype=jnp.int32), 0, NX - 1)
    bits = [(gz >> t) & 1 for t in range(4)]
    ones = [gz & 1, (gz & 3) == 3, (gz & 7) == 7]
    zeros = [(gz & 1) == 0, (gz & 3) == 0, (gz & 7) == 0]
    after = sum(jnp.asarray(v).astype(jnp.int32) for v in ones)
    before = sum(jnp.asarray(v).astype(jnp.int32) for v in zeros)
    info = jnp.stack([gz * ZS, 2 * grp] + bits + [before, after]).astype(jnp.int32)
    pay, win, low, high = call(
        project_kernel,
        (sds((64, 128), f32), sds((12, ZS, HALF), f32), sds((48, 128), f32), sds((48, 128), f32)),
        [SMEM] * 4 + [VMEM] * 3, [pltpu.VMEM((16, NY), f32)],
        10**7, 4 * 10**6, "project", VMEM, 8,
    )(info, tile_col, tile_subset_block, xs, pet_rows, mr_rows, tiles)
    got = []
    for step in range(4):
        got.append(lax.ppermute(pay, GZ, [(i, i ^ (2 ** (step + 1) - 1)) for i in range(16)]))
        if step == 0:
            kspace_data, got[0] = lax.optimization_barrier((kspace_data, got[0]))
        if step < 3:
            edge = jnp.where(bits[step + 1] == 1, low, high)
            pay = jnp.concatenate([pay[:16] + got[step][:16], edge], 0)
    data_own, data_out = call(
        prepare_kernel, (sds((3, 2 * NZ, HALF), bf16), sds((2, 2 * NZ, HALF), bf16)),
        [SMEM, VMEM, VMEM], [], 10**6, 3 * 10**6, "prepare", VMEM, 8,
    )(core_arr, kspace_data.transpose(0, 2, 3, 1), kspace_mask.T)
    data_got = lax.ppermute(data_out, "c", [(0, 1), (1, 0)])
    couple_pet, couple_mr = call(
        coupling_kernel, (sds((2, ZS, HALF), f32), sds((2, ZS, ROW), f32)),
        [SMEM] + [VMEM] * 5,
        [pltpu.VMEM((12, 24, HALF), f32), pltpu.VMEM((4, 24, HALF), f32),
         pltpu.VMEM((3, 16, HALF), f32)],
        10**6, 10**6, "coupling", VMEM, 8,
    )(info, win, *got)

    parts = call(
        coil_kernel, sds((8, 4 * ZS, ROW), bf16), [SMEM] * 4 + [ANY] * 10,
        [pltpu.VMEM((32, CHUNK, 128), bf16), pltpu.VMEM((ROW, ROW), bf16),
         pltpu.VMEM((2, 2 * NZ, 2 * NZ), bf16), pltpu.VMEM((2, 2, 2 * NZ, HALF), bf16),
         pltpu.VMEM((2 * NZ, HALF), bf16), pltpu.VMEM((16, NY, 128), bf16),
         pltpu.VMEM((2, 64, 128), f32), pltpu.VMEM((2, 64, 128), f32),
         pltpu.VMEM((16, 128), f32), pltpu.VMEM((16, 128), f32), pltpu.VMEM((4, ZS * NX, 128), f32),
         pltpu.VMEM((4 * NZ, ROW), f32), pltpu.VMEM((4 * NZ, ROW), bf16),
         pltpu.VMEM((4 * NZ, ROW), bf16), pltpu.VMEM((8, 4 * ZS, ROW), bf16),
         pltpu.SemaphoreType.DMA((20,)), pltpu.SemaphoreType.DMA((2,))],
        5 * 10**9, 6 * 10**6, "coils", ANY, 61,
    )(core_arr, tile_col, tile_subset_block, subset_view_blocks, recv, y_table(), z_tables(), data_own,
      data_got, tiles, pay, got[3], measured, background)

    both = lax.all_to_all(parts, ("x", "c"), split_axis=0, concat_axis=0, tiled=True)
    half = lax.axis_index("zh").astype(jnp.int32).reshape(1)
    mr_own, mr_other, pet_own, pet_other = call(
        sum_kernel,
        (sds((2 * ZS, ROW), bf16), sds((2 * ZS, ROW), bf16), sds((ZS, ROW), f32), sds((ZS, ROW), bf16)),
        [SMEM, VMEM], [], 10**6, 10**6, "sums",
    )(half, both)
    places = [(zh, p, j) for zh in range(2) for p in range(8) for j in range(16)]
    mr_a = lax.ppermute(
        mr_own, GRP + GZ, [((zh * 8 + p) * 16 + j, j * 16 + zh * 8 + p) for zh, p, j in places]
    )
    mr_b = lax.ppermute(
        mr_other, GRP + GZ, [((zh * 8 + p) * 16 + j, j * 16 + (1 - zh) * 8 + p) for zh, p, j in places]
    )
    pet_got = lax.ppermute(pet_other, "zh", [(0, 1), (1, 0)])
    return call(
        final_kernel, (sds((ZS, 2, NY), f32), sds((ZS, 2, 2 * NY), f32)), [VMEM] * 6, [],
        10**5, 10**6, "final",
    )(mr_a, mr_b, pet_own, pet_got, couple_pet, couple_mr)


def solution(mesh):
    fine = Mesh(mesh.devices.reshape(2, 4, 2, 4, 4), ("zh", "x", "c", "zl", "y"))
    placed = (
        P(GZ, None, None),
        P(GZ, None, None),
        P(GRP, GZ, None, None),
        P(GRP, None, GZ, None),
        P(),
        P(GRP + GZ, None, None),
        P(GRP + GZ),
        P(GRP + GZ),
        P(GRP, None),
        P(GRP, None),
        P(GRP),
    )
    return jax.shard_map(
        on_device,
        mesh=fine,
        in_specs=placed,
        out_specs=(P(GZ, GRP, None), P(GZ, GRP, None)),
        check_vma=False,
    )
```

```python
import math

import jax
import jax.numpy as jnp
import numpy as np
from jax import lax
from jax.experimental import pallas as pl
from jax.experimental.pallas import tpu as pltpu
from jax.sharding import Mesh, PartitionSpec as P

coupling_weight = 0.1
mag_smooth = 0.3
eta_smooth = 0.3

ZS, NX, NY, NZ = 8, 32, 480, 128
HALF = 512
ROW = 2 * HALF
CHUNK = 152
GRP = ("zh", "x", "c")
GZ = ("zl", "y")
f32, bf16 = jnp.float32, jnp.bfloat16

SMEM = pl.BlockSpec(memory_space=pltpu.SMEM)
VMEM = pl.BlockSpec(memory_space=pltpu.VMEM)
ANY = pl.BlockSpec(memory_space=pl.ANY)


def dft_parts(length):
    indices = np.arange(length)
    angles = (indices[:, None] * indices[None, :] % length) * (2.0 * math.pi / length)
    scaling = 1.0 / math.sqrt(length)
    return np.cos(angles) * scaling, -np.sin(angles) * scaling


def y_table():
    real_part, imag_part = dft_parts(NY)
    table = np.zeros((2, HALF, 2, HALF), np.float64)
    table[0, :NY, 0, :NY] = real_part
    table[0, :NY, 1, :NY] = imag_part
    table[1, :NY, 0, :NY] = -imag_part
    table[1, :NY, 1, :NY] = real_part
    return jnp.asarray(table.reshape(ROW, ROW).astype(jnp.bfloat16))


def arrived(slab):
    return slab % 4 * 4 + slab // 4


def z_tables():
    real_part, imag_part = dft_parts(NZ)
    table = np.block([[real_part, -imag_part], [imag_part, real_part]])
    place = np.arange(NZ)
    order = arrived(place // ZS) * ZS + place % ZS
    order = np.concatenate([order, NZ + order])
    return jnp.asarray(np.stack([table[:, order], table[order]]).astype(jnp.bfloat16))


def call(kernel, out_shape, in_specs, scratch, flops, moved, name, out_spec=VMEM, grant=40):
    return pl.pallas_call(
        kernel,
        out_shape=out_shape,
        in_specs=in_specs,
        out_specs=jax.tree.map(lambda _: out_spec, out_shape),
        scratch_shapes=scratch,
        compiler_params=pltpu.CompilerParams(vmem_limit_bytes=grant * 1024 * 1024),
        cost_estimate=pl.CostEstimate(flops=flops, bytes_accessed=moved, transcendentals=0),
        name=name,
    )


def pack_kernel(core_ref, sens_hbm, mr_hbm, out_hbm, sens_ref, mr_ref, order_ref, short_ref, rows_ref,
                mr_rows, out_ref, sems, out_sems):
    copies = []
    for n in range(4):
        part = pl.ds(128 * n, 128)
        copies.append(pltpu.make_async_copy(sens_hbm.at[part], sens_ref.at[part], sems.at[n]))
    for n in range(4):
        part = pl.ds(64 * n, 64)
        copies.append(pltpu.make_async_copy(mr_hbm.at[part], mr_ref.at[part], sems.at[4 + n]))
    for copy in copies:
        copy.start()
    for count, ref in ((2 * ZS, order_ref), (ZS, short_ref)):
        size = NX * count
        row = lax.broadcasted_iota(jnp.int32, (size, size), 0)
        col = lax.broadcasted_iota(jnp.int32, (size, size), 1)
        place, q = row // count, row % count
        source = q * NX + 2 * (place % 4 * 4 + place % 16 // 4) + place // 16
        ref[...] = jnp.where(col == source, 1.0, 0.0).astype(bf16)
    imag = core_ref[0] == 1
    rows_ref[256:, HALF + NY :] = jnp.zeros((256, HALF - NY), bf16)
    out_copies = []

    def send(rows):
        place = (slice(None), rows)
        copy = pltpu.make_async_copy(out_ref.at[place], out_hbm.at[place], out_sems.at[len(out_copies)])
        copy.start()
        out_copies.append(copy)

    for n in range(4):
        copies[n].wait()
        part = pl.ds(128 * n, 128)
        rows_ref[part, :NY] = sens_ref[part, :NY]
        rows_ref[part, HALF : HALF + NY] = sens_ref[part, NY:]
    for n in range(4):
        copies[4 + n].wait()
        part = pl.ds(64 * n, 64)
        values = jnp.where(imag, mr_ref[part, NY:], mr_ref[part, :NY]).astype(bf16)
        mr_rows[part, :] = values[:, :384]
        rows_ref[part, NY:HALF] = values[:, 384:416]
        rows_ref[pl.ds(256 + 64 * n, 64), NY:HALF] = values[:, 416:448]
        rows_ref[part, HALF + NY :] = values[:, 448:]
    for n in range(4):
        moved = jnp.dot(order_ref[...], rows_ref[:, 256 * n : 256 * (n + 1)], preferred_element_type=f32)
        for b in range(2):
            first = 16 * (2 * n + b)
            block = moved[:, 128 * b : 128 * (b + 1)].astype(bf16)
            out_ref[:, first : first + 16, :] = block.reshape(NX, 16, 128)
        send(pl.ds(32 * n, 32))
    moved = jnp.dot(short_ref[...], mr_rows[...], preferred_element_type=f32)
    blocks = [moved[:, 128 * b : 128 * (b + 1)].reshape(NX, ZS, 128) for b in range(3)]
    out_ref[:, 128:, :] = jnp.concatenate(blocks, 1).astype(bf16)
    send(pl.ds(128, CHUNK - 128))
    for copy in out_copies:
        copy.wait()


def prepare_kernel(core_ref, data_ref, mask_ref, own_out, other_out):
    pad = jnp.zeros((HALF - NY, NZ), f32)

    def turned(values):
        return jnp.concatenate([values.astype(f32), pad], 0).T.astype(bf16)

    for k in range(2):
        for place, out in ((core_ref[0], own_out), (1 - core_ref[0], other_out)):
            for part in range(2):
                values = data_ref[k, place, part * NY : (part + 1) * NY, :]
                out[k, part * NZ : (part + 1) * NZ, :] = turned(values)
    own_out[2, :NZ, :] = turned(mask_ref[...])
    own_out[2, NZ:, :] = jnp.zeros((NZ, HALF), bf16)


def project_kernel(
    info_ref, col_ref, block_ref, xs_ref, pet_ref, mr_ref, tiles_ref,
    pay_ref, win_ref, low_ref, high_ref, picked,
):
    for t in range(16):
        picked[pl.ds(t, 1), :] = pet_ref[pl.ds(col_ref[t], 1), :]
    rows = picked[...].astype(bf16)
    pay_ref[:16, :] = jnp.zeros((16, 128), f32)
    for t in range(16):
        product = jnp.dot(rows, tiles_ref[t], preferred_element_type=f32)
        place = pl.ds(block_ref[t], 1)
        pay_ref[place, :] = pay_ref[place, :] + product[t : t + 1, :]
    win_ref[...] = jnp.zeros((12, ZS, HALF), f32)
    for r in range(4):
        for z in range(ZS):
            place = pl.ds(xs_ref[r] + z * NX, 1)
            win_ref[r, z : z + 1, :NY] = pet_ref[place, :]
            win_ref[4 + r, z : z + 1, :NY] = mr_ref[place, :NY]
            win_ref[8 + r, z : z + 1, :NY] = mr_ref[place, NY:]
    for b in range(4):
        for r in range(12):
            row = pl.ds(12 * b + r, 1)
            low_ref[row, :] = win_ref[r, 0:1, 128 * b : 128 * (b + 1)]
            high_ref[row, :] = win_ref[r, ZS - 1 : ZS, 128 * b : 128 * (b + 1)]
    pay_ref[16:, :] = jnp.where(info_ref[2] == 1, low_ref[...], high_ref[...])


def ratio_rows(block_ref, view_ref, pay_ref, got_ref, measured_ref, background_ref, ratio, gathered):
    for j in range(16):
        counts = measured_ref[pl.ds(view_ref[j], 1), :]
        back = background_ref[pl.ds(view_ref[j], 1), :]
        projection = (pay_ref[j : j + 1, :] + got_ref[j : j + 1, :]) / NY
        ratio[j : j + 1, :] = 1.0 - counts / (projection + back)
    for t in range(16):
        gathered[t : t + 1, :] = ratio[pl.ds(block_ref[t], 1), :]
    return gathered[...].astype(bf16)


def backproject(col_ref, rows, tiles_ref, acc, out_ref):
    acc[...] = jnp.zeros((4, ZS * NX, 128), f32)
    for t in range(16):
        spread = lax.dot_general(
            rows, tiles_ref[t], (((1,), (1,)), ((), ())), preferred_element_type=f32
        )
        place = pl.ds(col_ref[t], 1)
        for b in range(4):
            block = spread[t : t + 1, 128 * b : min(128 * (b + 1), NY)]
            lanes = slice(0, block.shape[1])
            acc[b, place, lanes] = acc[b, place, lanes] + block
    for p in range(16):
        rows_out = slice((2 + p // 8) * ZS, (3 + p // 8) * ZS)
        for k in range(2):
            for b in range(4):
                block = acc[b, pl.ds(2 * p + k, ZS, stride=NX), :] / NY
                first = k * HALF + 128 * b
                out_ref[p % 8, rows_out, first : first + 128] = block.astype(bf16)


def coupling_kernel(
    info_ref, win_ref, got_a, got_b, got_c, got_d, pet_out, mr_out, planes, mags, moved
):
    z_start, x_first = info_ref[0], info_ref[1]
    edges = []
    for which in (info_ref[6], info_ref[7]):
        edge = got_d[16:, :]
        for step, got in enumerate((got_a, got_b, got_c)):
            edge = jnp.where(which == step, got[16:, :], edge)
        edges.append(edge)
    planes[...] = jnp.zeros((12, 24, HALF), f32)
    for r in range(12):
        planes[r, 1 : ZS + 1, :] = win_ref[r]
        for b in range(4):
            lanes = slice(128 * b, 128 * (b + 1))
            planes[r, 0:1, lanes] = edges[0][12 * b + r : 12 * b + r + 1, :]
            planes[r, ZS + 1 : ZS + 2, lanes] = edges[1][12 * b + r : 12 * b + r + 1, :]
    for r in range(4):
        mags[r] = jnp.sqrt(planes[4 + r] ** 2 + planes[8 + r] ** 2 + mag_smooth**2)
    shape = (16, HALF)
    level = z_start - 1 + lax.broadcasted_iota(jnp.int32, shape, 0)
    lane = lax.broadcasted_iota(jnp.int32, shape, 1)
    step_z = level < NZ - 1
    step_y = lane < NY - 1
    term_z = (level >= 0) & (lane < NY)

    def differences(ref, r, step_x):
        here = ref[r, 0:16, :]
        along_z = jnp.where(step_z, ref[r, 1:17, :] - here, 0.0)
        along_x = jnp.where(step_x, ref[r + 1, 0:16, :] - here, 0.0)
        along_y = jnp.where(step_y, pltpu.roll(here, HALF - 1, 1) - here, 0.0)
        return along_z, along_x, along_y

    grads = []
    for r in range(3):
        place = x_first - 1 + r
        step_x = place < NX - 1
        a = differences(planes, r, step_x)
        b = differences(mags, r, step_x)
        a_sq = a[0] ** 2 + a[1] ** 2 + a[2] ** 2
        b_sq = b[0] ** 2 + b[1] ** 2 + b[2] ** 2
        cross = a[0] * b[0] + a[1] * b[1] + a[2] * b[2]
        weight = lax.rsqrt(eta_smooth**2 + a_sq * b_sq - cross * cross)
        weight = jnp.where(term_z & (place >= 0), weight, 0.0)
        grads.append(
            (
                [(p * b_sq - q * cross) * weight for p, q in zip(a, b)],
                [(q * a_sq - p * cross) * weight for p, q in zip(a, b)],
            )
        )

    for k in range(2):
        found = []
        for which in range(2):
            here, before = grads[k + 1][which], grads[k][which]
            total = before[1] - here[0] - here[1] - here[2]
            total = total + pltpu.roll(here[0], 1, 0) + pltpu.roll(here[2], 1, 1)
            found.append(coupling_weight * total)
        moved[0] = found[0]
        scaled = found[1] / mags[k + 1, 0:16, :]
        moved[1] = scaled * planes[5 + k, 0:16, :]
        moved[2] = scaled * planes[9 + k, 0:16, :]
        pet_out[k] = moved[0, 1 : ZS + 1, :]
        mr_out[k, :, :HALF] = moved[1, 1 : ZS + 1, :]
        mr_out[k, :, HALF:] = moved[2, 1 : ZS + 1, :]


def coil_kernel(core_ref, col_ref, block_ref, view_ref, recv_hbm, ytab_hbm, ztab_hbm, data_own_hbm,
                data_got_hbm, tiles_hbm, pay_hbm, got_hbm, measured_hbm, background_hbm,
                out_hbm, recv_ref, ytab_ref, ztab_ref, data_ref, mask_ref, tiles_ref, bins_ref, counts_ref,
                ratio, gathered, acc, sens, images, kyrows, out_ref, sems, out_sems):
    copies = []

    def fetch(source, target):
        copies.append(pltpu.make_async_copy(source, target, sems.at[len(copies)]))
        copies[-1].start()
        return copies[-1]

    small = [
        fetch(pay_hbm, bins_ref.at[0]), fetch(got_hbm, bins_ref.at[1]),
        fetch(measured_hbm, counts_ref.at[0]), fetch(background_hbm, counts_ref.at[1]),
    ]
    received = [fetch(recv_hbm.at[pl.ds(8 * n, 8)], recv_ref.at[pl.ds(8 * n, 8)]) for n in range(4)]
    tables = [
        fetch(ytab_hbm.at[pl.ds(256 * n, 256)], ytab_ref.at[pl.ds(256 * n, 256)]) for n in range(4)
    ]
    others = [
        fetch(ztab_hbm, ztab_ref),
        fetch(data_own_hbm.at[pl.ds(0, 2)], data_ref.at[core_ref[0]]),
        fetch(data_got_hbm, data_ref.at[1 - core_ref[0]]),
        fetch(data_own_hbm.at[2], mask_ref),
    ]
    tiles = [fetch(tiles_hbm.at[pl.ds(4 * n, 4)], tiles_ref.at[pl.ds(4 * n, 4)]) for n in range(4)]
    for copy in small:
        copy.wait()
    ratio_now = ratio_rows(
        block_ref, view_ref, bins_ref.at[0], bins_ref.at[1], counts_ref.at[0], counts_ref.at[1], ratio, gathered
    )
    for copy in received:
        copy.wait()

    def block(c, b):
        return recv_ref[16 * c : 16 * (c + 1), 16 * b : 16 * (b + 1), :].astype(f32)

    lane = lax.broadcasted_iota(jnp.int32, (NZ, 128), 1)

    def image_part(c):
        tail = recv_ref[16 * c : 16 * (c + 1), 128:, :].astype(f32)
        parts = [tail[:, ZS * b : ZS * (b + 1)].reshape(NZ, 128) for b in range(3)]
        real, imag = block(c, 3), block(c, 7)
        first = pltpu.roll(real[:, :ZS].reshape(NZ, 128), 32, 1)
        second = pltpu.roll(real[:, ZS:].reshape(NZ, 128), 64, 1)
        third = pltpu.roll(imag[:, :ZS].reshape(NZ, 128), 96, 1)
        last = jnp.where(lane < 32, first, jnp.where(lane < 64, second, third))
        return jnp.concatenate(parts + [jnp.where(lane < 96, last, 0.0)], -1)

    mr_re, mr_im = image_part(0), image_part(1)
    for c in range(2):
        for b in range(4):
            real, imag = block(c, b), block(c, 4 + b)
            lanes = slice(128 * b, 128 * (b + 1))
            lanes_im = slice(HALF + 128 * b, HALF + 128 * (b + 1))
            for k in range(2):
                rows = pl.ds((2 * c + k) * NZ, NZ)
                s_re = real[:, k * ZS : (k + 1) * ZS].reshape(NZ, 128)
                s_im = imag[:, k * ZS : (k + 1) * ZS].reshape(NZ, 128)
                sens[rows, lanes] = s_re
                sens[rows, lanes_im] = s_im
                images[rows, lanes] = (s_re * mr_re[:, lanes] - s_im * mr_im[:, lanes]).astype(bf16)
                images[rows, lanes_im] = (s_re * mr_im[:, lanes] + s_im * mr_re[:, lanes]).astype(bf16)
    for copy in tables:
        copy.wait()
    kyrows[...] = jnp.dot(images[...], ytab_ref[...], preferred_element_type=f32).astype(bf16)
    for copy in others:
        copy.wait()
    mask = mask_ref[:NZ, :].astype(f32)
    for q in range(4):
        rows = pl.ds(q * NZ, NZ)
        volume = jnp.concatenate([kyrows[rows, :HALF], kyrows[rows, HALF:]], 0)
        kspace = jnp.dot(ztab_ref[0], volume, preferred_element_type=f32)
        data = data_ref[q // 2, q % 2].astype(f32)
        misfit = jnp.concatenate(
            [mask * (kspace[:NZ] - data[:NZ]), mask * (data[NZ:] - kspace[NZ:])], 0
        ).astype(bf16)
        back = jnp.dot(ztab_ref[1], misfit, preferred_element_type=f32).astype(bf16)
        images[rows, :HALF] = back[:NZ]
        images[rows, HALF:] = back[NZ:]
    for copy in tiles:
        copy.wait()
    backproject(col_ref, ratio_now, tiles_ref, acc, out_ref)
    out_copies = []
    for n in (1, 0):
        part = (slice(None), pl.ds(2 * ZS * n, 2 * ZS))
        out_copies.append(pltpu.make_async_copy(out_ref.at[part], out_hbm.at[part], out_sems.at[n]))
    out_copies[0].start()
    for b in range(4):
        lanes = slice(128 * b, 128 * (b + 1))
        lanes_im = slice(HALF + 128 * b, HALF + 128 * (b + 1))
        table = jnp.concatenate([ytab_ref[:, lanes], ytab_ref[:, lanes_im]], 1)
        image = jnp.dot(images[...], table, preferred_element_type=f32)
        total_re = jnp.zeros((NZ, 128), f32)
        total_im = jnp.zeros((NZ, 128), f32)
        for q in range(4):
            rows = slice(q * NZ, (q + 1) * NZ)
            s_re, s_im = sens[rows, lanes], sens[rows, lanes_im]
            i_re, i_im = image[rows, :128], image[rows, 128:]
            total_re = total_re + (s_re * i_re - s_im * i_im)
            total_im = total_im - (s_re * i_im + s_im * i_re)
        for total, place in ((total_re, lanes), (total_im, lanes_im)):
            slabs = total.reshape(16, ZS, 128)
            for p in range(8):
                both = jnp.concatenate([slabs[arrived(2 * p)], slabs[arrived(2 * p + 1)]], 0)
                out_ref[p, : 2 * ZS, place] = both.astype(bf16)
    out_copies[1].start()
    for copy in out_copies:
        copy.wait()


def sum_kernel(half_ref, recv_ref, mr_own, mr_other, pet_own, pet_other):
    upper = half_ref[0] == 1
    pet = jnp.zeros((2 * ZS, ROW), f32)
    for c in range(2):
        mr = jnp.zeros((2 * ZS, ROW), f32)
        for x in range(4):
            block = recv_ref[2 * x + c].astype(f32)
            mr = mr + block[: 2 * ZS]
            pet = pet + block[2 * ZS :]
        rows = pl.ds(c * ZS, ZS)
        mr_own[rows, :] = jnp.where(upper, mr[ZS:], mr[:ZS]).astype(bf16)
        mr_other[rows, :] = jnp.where(upper, mr[:ZS], mr[ZS:]).astype(bf16)
    pet_own[...] = jnp.where(upper, pet[ZS:], pet[:ZS])
    pet_other[...] = jnp.where(upper, pet[:ZS], pet[ZS:]).astype(bf16)


def final_kernel(mr_a, mr_b, pet_a, pet_b, couple_pet_ref, couple_mr_ref, pet_out, mr_out):
    for k in range(2):
        rows = pl.ds(k * ZS, ZS)
        lanes = pl.ds(k * HALF, HALF)
        pet = pet_a[:, lanes] + pet_b[:, lanes].astype(f32) + couple_pet_ref[k]
        mr = mr_a[rows, :].astype(f32) + mr_b[rows, :].astype(f32) + couple_mr_ref[k]
        pet_out[:, k, :] = pet[:, :NY]
        mr_out[:, k, :NY] = mr[:, :NY]
        mr_out[:, k, NY:] = mr[:, HALF : HALF + NY]


def sds(shape, dtype):
    return jax.ShapeDtypeStruct(shape, dtype)


def on_device(
    pet_image, mr_image, coil_sens, kspace_data, kspace_mask, system_tiles,
    tile_subset_block, tile_col, measured, background, subset_view_blocks,
):
    core = lax.axis_index("c")
    grp = lax.axis_index(GRP)
    gz = lax.axis_index(GZ)
    core_arr = core.astype(jnp.int32).reshape(1)
    pet_rows = pet_image.reshape(ZS * NX, NY)
    mr_rows = mr_image.reshape(ZS * NX, 2 * NY)
    tiles = system_tiles.swapaxes(1, 2)

    sent = call(
        pack_kernel, sds((32, CHUNK, 128), bf16), [SMEM] + [ANY] * 2,
        [pltpu.VMEM((2 * ZS * NX, 2 * NY), bf16), pltpu.VMEM((ZS * NX, 2 * NY), f32),
         pltpu.VMEM((512, 512), bf16), pltpu.VMEM((256, 256), bf16), pltpu.VMEM((512, ROW), bf16),
         pltpu.VMEM((256, 384), bf16), pltpu.VMEM((32, CHUNK, 128), bf16),
         pltpu.SemaphoreType.DMA((8,)), pltpu.SemaphoreType.DMA((5,))],
        10**9, 4 * 10**6, "pack", ANY, 60,
    )(core_arr, coil_sens.reshape(2 * ZS * NX, 2 * NY), mr_rows)
    sent, tile_col = lax.optimization_barrier((sent, tile_col))
    recv = lax.all_to_all(sent, ("c", "y", "zl"), split_axis=0, concat_axis=0, tiled=True)

    xs = jnp.clip(2 * grp - 1 + jnp.arange(4, dtype=jnp.int32), 0, NX - 1)
    bits = [(gz >> t) & 1 for t in range(4)]
    ones = [gz & 1, (gz & 3) == 3, (gz & 7) == 7]
    zeros = [(gz & 1) == 0, (gz & 3) == 0, (gz & 7) == 0]
    after = sum(jnp.asarray(v).astype(jnp.int32) for v in ones)
    before = sum(jnp.asarray(v).astype(jnp.int32) for v in zeros)
    info = jnp.stack([gz * ZS, 2 * grp] + bits + [before, after]).astype(jnp.int32)
    pay, win, low, high = call(
        project_kernel,
        (sds((64, 128), f32), sds((12, ZS, HALF), f32), sds((48, 128), f32), sds((48, 128), f32)),
        [SMEM] * 4 + [VMEM] * 3, [pltpu.VMEM((16, NY), f32)],
        10**7, 4 * 10**6, "project", VMEM, 8,
    )(info, tile_col, tile_subset_block, xs, pet_rows, mr_rows, tiles)
    got = []
    for step in range(4):
        got.append(lax.ppermute(pay, GZ, [(i, i ^ (2 ** (step + 1) - 1)) for i in range(16)]))
        if step == 0:
            kspace_data, got[0] = lax.optimization_barrier((kspace_data, got[0]))
        if step < 3:
            edge = jnp.where(bits[step + 1] == 1, low, high)
            pay = jnp.concatenate([pay[:16] + got[step][:16], edge], 0)
    data_own, data_out = call(
        prepare_kernel, (sds((3, 2 * NZ, HALF), bf16), sds((2, 2 * NZ, HALF), bf16)),
        [SMEM, VMEM, VMEM], [], 10**6, 3 * 10**6, "prepare", VMEM, 8,
    )(core_arr, kspace_data.transpose(0, 2, 3, 1), kspace_mask.T)
    data_got = lax.ppermute(data_out, "c", [(0, 1), (1, 0)])
    couple_pet, couple_mr = call(
        coupling_kernel, (sds((2, ZS, HALF), f32), sds((2, ZS, ROW), f32)),
        [SMEM] + [VMEM] * 5,
        [pltpu.VMEM((12, 24, HALF), f32), pltpu.VMEM((4, 24, HALF), f32),
         pltpu.VMEM((3, 16, HALF), f32)],
        10**6, 10**6, "coupling", VMEM, 8,
    )(info, win, *got)

    parts = call(
        coil_kernel, sds((8, 4 * ZS, ROW), bf16), [SMEM] * 4 + [ANY] * 10,
        [pltpu.VMEM((32, CHUNK, 128), bf16), pltpu.VMEM((ROW, ROW), bf16),
         pltpu.VMEM((2, 2 * NZ, 2 * NZ), bf16), pltpu.VMEM((2, 2, 2 * NZ, HALF), bf16),
         pltpu.VMEM((2 * NZ, HALF), bf16), pltpu.VMEM((16, NY, 128), bf16),
         pltpu.VMEM((2, 64, 128), f32), pltpu.VMEM((2, 64, 128), f32),
         pltpu.VMEM((16, 128), f32), pltpu.VMEM((16, 128), f32), pltpu.VMEM((4, ZS * NX, 128), f32),
         pltpu.VMEM((4 * NZ, ROW), f32), pltpu.VMEM((4 * NZ, ROW), bf16),
         pltpu.VMEM((4 * NZ, ROW), bf16), pltpu.VMEM((8, 4 * ZS, ROW), bf16),
         pltpu.SemaphoreType.DMA((20,)), pltpu.SemaphoreType.DMA((2,))],
        5 * 10**9, 6 * 10**6, "coils", ANY, 61,
    )(core_arr, tile_col, tile_subset_block, subset_view_blocks, recv, y_table(), z_tables(), data_own,
      data_got, tiles, pay, got[3], measured, background)

    both = lax.all_to_all(parts, ("x", "c"), split_axis=0, concat_axis=0, tiled=True)
    half = lax.axis_index("zh").astype(jnp.int32).reshape(1)
    mr_own, mr_other, pet_own, pet_other = call(
        sum_kernel,
        (sds((2 * ZS, ROW), bf16), sds((2 * ZS, ROW), bf16), sds((ZS, ROW), f32), sds((ZS, ROW), bf16)),
        [SMEM, VMEM], [], 10**6, 10**6, "sums",
    )(half, both)
    places = [(zh, p, j) for zh in range(2) for p in range(8) for j in range(16)]
    mr_a = lax.ppermute(
        mr_own, GRP + GZ, [((zh * 8 + p) * 16 + j, j * 16 + 2 * p + 1 * zh) for zh, p, j in places]
    )
    mr_b = lax.ppermute(
        mr_other, GRP + GZ, [((zh * 8 + p) * 16 + j, j * 16 + 2 * p + 1 * (1 - zh)) for zh, p, j in places]
    )
    pet_got = lax.ppermute(pet_other, "zh", [(0, 1), (1, 0)])
    return call(
        final_kernel, (sds((ZS, 2, NY), f32), sds((ZS, 2, 2 * NY), f32)), [VMEM] * 6, [],
        10**5, 10**6, "final",
    )(mr_a, mr_b, pet_own, pet_got, couple_pet, couple_mr)


def solution(mesh):
    fine = Mesh(mesh.devices.reshape(2, 4, 2, 4, 4), ("zh", "x", "c", "zl", "y"))
    placed = (
        P(GZ, None, None),
        P(GZ, None, None),
        P(GRP, GZ, None, None),
        P(GRP, None, GZ, None),
        P(),
        P(GRP + GZ, None, None),
        P(GRP + GZ),
        P(GRP + GZ),
        P(GRP, None),
        P(GRP, None),
        P(GRP),
    )
    return jax.shard_map(
        on_device,
        mesh=fine,
        in_specs=placed,
        out_specs=(P(GZ, GRP, None), P(GZ, GRP, None)),
        check_vma=False,
    )
```

```python
import math

import jax
import jax.numpy as jnp
import numpy as np
from jax import lax
from jax.experimental import pallas as pl
from jax.experimental.pallas import tpu as pltpu
from jax.sharding import Mesh, PartitionSpec as P

coupling_weight = 0.1
mag_smooth = 0.3
eta_smooth = 0.3

ZS, NX, NY, NZ = 8, 32, 480, 128
HALF = 512
ROW = 2 * HALF
CHUNK = 152
GRP = ("zh", "x", "c")
GZ = ("zl", "y")
f32, bf16 = jnp.float32, jnp.bfloat16

SMEM = pl.BlockSpec(memory_space=pltpu.SMEM)
VMEM = pl.BlockSpec(memory_space=pltpu.VMEM)
ANY = pl.BlockSpec(memory_space=pl.ANY)


def dft_parts(length):
    indices = np.arange(length)
    angles = (indices[:, None] * indices[None, :] % length) * (2.0 * math.pi / length)
    scaling = 1.0 / math.sqrt(length)
    return np.cos(angles) * scaling, -np.sin(angles) * scaling


def y_table():
    real_part, imag_part = dft_parts(NY)
    table = np.zeros((2, HALF, 2, HALF), np.float64)
    table[0, :NY, 0, :NY] = real_part
    table[0, :NY, 1, :NY] = imag_part
    table[1, :NY, 0, :NY] = -imag_part
    table[1, :NY, 1, :NY] = real_part
    return jnp.asarray(table.reshape(ROW, ROW).astype(jnp.bfloat16))


def arrived(slab):
    return slab % 4 * 4 + slab // 4


def z_tables():
    real_part, imag_part = dft_parts(NZ)
    table = np.block([[real_part, -imag_part], [imag_part, real_part]])
    place = np.arange(NZ)
    order = arrived(place // ZS) * ZS + place % ZS
    order = np.concatenate([order, NZ + order])
    return jnp.asarray(np.stack([table[:, order], table[order]]).astype(jnp.bfloat16))


def call(kernel, out_shape, in_specs, scratch, flops, moved, name, out_spec=VMEM, grant=40):
    return pl.pallas_call(
        kernel,
        out_shape=out_shape,
        in_specs=in_specs,
        out_specs=jax.tree.map(lambda _: out_spec, out_shape),
        scratch_shapes=scratch,
        compiler_params=pltpu.CompilerParams(vmem_limit_bytes=grant * 1024 * 1024),
        cost_estimate=pl.CostEstimate(flops=flops, bytes_accessed=moved, transcendentals=0),
        name=name,
    )


def pack_kernel(core_ref, sens_hbm, mr_hbm, out_hbm, sens_ref, mr_ref, order_ref, short_ref, rows_ref,
                mr_rows, out_ref, sems, out_sems):
    copies = []
    for n in range(4):
        part = pl.ds(128 * n, 128)
        copies.append(pltpu.make_async_copy(sens_hbm.at[part], sens_ref.at[part], sems.at[n]))
    for n in range(4):
        part = pl.ds(64 * n, 64)
        copies.append(pltpu.make_async_copy(mr_hbm.at[part], mr_ref.at[part], sems.at[4 + n]))
    for copy in copies:
        copy.start()
    for count, ref in ((2 * ZS, order_ref), (ZS, short_ref)):
        size = NX * count
        row = lax.broadcasted_iota(jnp.int32, (size, size), 0)
        col = lax.broadcasted_iota(jnp.int32, (size, size), 1)
        place, q = row // count, row % count
        source = q * NX + 2 * (place % 4 * 4 + place % 16 // 4) + place // 16
        ref[...] = jnp.where(col == source, 1.0, 0.0).astype(bf16)
    imag = core_ref[0] == 1
    rows_ref[256:, HALF + NY :] = jnp.zeros((256, HALF - NY), bf16)
    out_copies = []

    def send(rows):
        place = (slice(None), rows)
        copy = pltpu.make_async_copy(out_ref.at[place], out_hbm.at[place], out_sems.at[len(out_copies)])
        copy.start()
        out_copies.append(copy)

    for n in range(4):
        copies[n].wait()
        part = pl.ds(128 * n, 128)
        rows_ref[part, :NY] = sens_ref[part, :NY]
        rows_ref[part, HALF : HALF + NY] = sens_ref[part, NY:]
    for n in range(4):
        copies[4 + n].wait()
        part = pl.ds(64 * n, 64)
        values = jnp.where(imag, mr_ref[part, NY:], mr_ref[part, :NY]).astype(bf16)
        mr_rows[part, :] = values[:, :384]
        rows_ref[part, NY:HALF] = values[:, 384:416]
        rows_ref[pl.ds(256 + 64 * n, 64), NY:HALF] = values[:, 416:448]
        rows_ref[part, HALF + NY :] = values[:, 448:]
    for n in range(4):
        moved = jnp.dot(order_ref[...], rows_ref[:, 256 * n : 256 * (n + 1)], preferred_element_type=f32)
        for b in range(2):
            first = 16 * (2 * n + b)
            block = moved[:, 128 * b : 128 * (b + 1)].astype(bf16)
            out_ref[:, first : first + 16, :] = block.reshape(NX, 16, 128)
        send(pl.ds(32 * n, 32))
    moved = jnp.dot(short_ref[...], mr_rows[...], preferred_element_type=f32)
    blocks = [moved[:, 128 * b : 128 * (b + 1)].reshape(NX, ZS, 128) for b in range(3)]
    out_ref[:, 128:, :] = jnp.concatenate(blocks, 1).astype(bf16)
    send(pl.ds(128, CHUNK - 128))
    for copy in out_copies:
        copy.wait()


def prepare_kernel(core_ref, data_ref, mask_ref, own_out, other_out):
    pad = jnp.zeros((HALF - NY, NZ), f32)

    def turned(values):
        return jnp.concatenate([values.astype(f32), pad], 0).T.astype(bf16)

    for k in range(2):
        for place, out in ((core_ref[0], own_out), (1 - core_ref[0], other_out)):
            for part in range(2):
                values = data_ref[k, place, part * NY : (part + 1) * NY, :]
                out[k, part * NZ : (part + 1) * NZ, :] = turned(values)
    own_out[2, :NZ, :] = turned(mask_ref[...])
    own_out[2, NZ:, :] = jnp.zeros((NZ, HALF), bf16)


def project_kernel(
    info_ref, col_ref, block_ref, xs_ref, pet_ref, mr_ref, tiles_ref,
    pay_ref, win_ref, low_ref, high_ref, picked,
):
    for t in range(16):
        picked[pl.ds(t, 1), :] = pet_ref[pl.ds(col_ref[t], 1), :]
    rows = picked[...].astype(bf16)
    pay_ref[:16, :] = jnp.zeros((16, 128), f32)
    for t in range(16):
        product = jnp.dot(rows, tiles_ref[t], preferred_element_type=f32)
        place = pl.ds(block_ref[t], 1)
        pay_ref[place, :] = pay_ref[place, :] + product[t : t + 1, :]
    win_ref[...] = jnp.zeros((12, ZS, HALF), f32)
    for r in range(4):
        for z in range(ZS):
            place = pl.ds(xs_ref[r] + z * NX, 1)
            win_ref[r, z : z + 1, :NY] = pet_ref[place, :]
            win_ref[4 + r, z : z + 1, :NY] = mr_ref[place, :NY]
            win_ref[8 + r, z : z + 1, :NY] = mr_ref[place, NY:]
    for b in range(4):
        for r in range(12):
            row = pl.ds(12 * b + r, 1)
            low_ref[row, :] = win_ref[r, 0:1, 128 * b : 128 * (b + 1)]
            high_ref[row, :] = win_ref[r, ZS - 1 : ZS, 128 * b : 128 * (b + 1)]
    pay_ref[16:, :] = jnp.where(info_ref[2] == 1, low_ref[...], high_ref[...])


def ratio_rows(block_ref, view_ref, pay_ref, got_ref, measured_ref, background_ref, ratio, gathered):
    for j in range(16):
        counts = measured_ref[pl.ds(view_ref[j], 1), :]
        back = background_ref[pl.ds(view_ref[j], 1), :]
        projection = (pay_ref[j : j + 1, :] + got_ref[j : j + 1, :]) / NY
        ratio[j : j + 1, :] = 1.0 - counts / (projection + back)
    for t in range(16):
        gathered[t : t + 1, :] = ratio[pl.ds(block_ref[t], 1), :]
    return gathered[...].astype(bf16)


def backproject(col_ref, rows, tiles_ref, acc, out_ref):
    acc[...] = jnp.zeros((4, ZS * NX, 128), f32)
    for t in range(16):
        spread = lax.dot_general(
            rows, tiles_ref[t], (((1,), (1,)), ((), ())), preferred_element_type=f32
        )
        place = pl.ds(col_ref[t], 1)
        for b in range(4):
            block = spread[t : t + 1, 128 * b : min(128 * (b + 1), NY)]
            lanes = slice(0, block.shape[1])
            acc[b, place, lanes] = acc[b, place, lanes] + block
    for p in range(16):
        rows_out = slice((2 + p // 8) * ZS, (3 + p // 8) * ZS)
        for k in range(2):
            for b in range(4):
                block = acc[b, pl.ds(2 * p + k, ZS, stride=NX), :] / NY
                first = k * HALF + 128 * b
                out_ref[p % 8, rows_out, first : first + 128] = block.astype(bf16)


def coupling_kernel(
    info_ref, win_ref, got_a, got_b, got_c, got_d, pet_out, mr_out, planes, mags, moved
):
    z_start, x_first = info_ref[0], info_ref[1]
    edges = []
    for which in (info_ref[6], info_ref[7]):
        edge = got_d[16:, :]
        for step, got in enumerate((got_a, got_b, got_c)):
            edge = jnp.where(which == step, got[16:, :], edge)
        edges.append(edge)
    planes[...] = jnp.zeros((12, 24, HALF), f32)
    for r in range(12):
        planes[r, 1 : ZS + 1, :] = win_ref[r]
        for b in range(4):
            lanes = slice(128 * b, 128 * (b + 1))
            planes[r, 0:1, lanes] = edges[0][12 * b + r : 12 * b + r + 1, :]
            planes[r, ZS + 1 : ZS + 2, lanes] = edges[1][12 * b + r : 12 * b + r + 1, :]
    for r in range(4):
        mags[r] = jnp.sqrt(planes[4 + r] ** 2 + planes[8 + r] ** 2 + mag_smooth**2)
    shape = (16, HALF)
    level = z_start - 1 + lax.broadcasted_iota(jnp.int32, shape, 0)
    lane = lax.broadcasted_iota(jnp.int32, shape, 1)
    step_z = level < NZ - 1
    step_y = lane < NY - 1
    term_z = (level >= 0) & (lane < NY)

    def differences(ref, r, step_x):
        here = ref[r, 0:16, :]
        along_z = jnp.where(step_z, ref[r, 1:17, :] - here, 0.0)
        along_x = jnp.where(step_x, ref[r + 1, 0:16, :] - here, 0.0)
        along_y = jnp.where(step_y, pltpu.roll(here, HALF - 1, 1) - here, 0.0)
        return along_z, along_x, along_y

    grads = []
    for r in range(3):
        place = x_first - 1 + r
        step_x = place < NX - 1
        a = differences(planes, r, step_x)
        b = differences(mags, r, step_x)
        a_sq = a[0] ** 2 + a[1] ** 2 + a[2] ** 2
        b_sq = b[0] ** 2 + b[1] ** 2 + b[2] ** 2
        cross = a[0] * b[0] + a[1] * b[1] + a[2] * b[2]
        weight = lax.rsqrt(eta_smooth**2 + a_sq * b_sq - cross * cross)
        weight = jnp.where(term_z & (place >= 0), weight, 0.0)
        grads.append(
            (
                [(p * b_sq - q * cross) * weight for p, q in zip(a, b)],
                [(q * a_sq - p * cross) * weight for p, q in zip(a, b)],
            )
        )

    for k in range(2):
        found = []
        for which in range(2):
            here, before = grads[k + 1][which], grads[k][which]
            total = before[1] - here[0] - here[1] - here[2]
            total = total + pltpu.roll(here[0], 1, 0) + pltpu.roll(here[2], 1, 1)
            found.append(coupling_weight * total)
        moved[0] = found[0]
        scaled = found[1] / mags[k + 1, 0:16, :]
        moved[1] = scaled * planes[5 + k, 0:16, :]
        moved[2] = scaled * planes[9 + k, 0:16, :]
        pet_out[k] = moved[0, 1 : ZS + 1, :]
        mr_out[k, :, :HALF] = moved[1, 1 : ZS + 1, :]
        mr_out[k, :, HALF:] = moved[2, 1 : ZS + 1, :]


def coil_kernel(core_ref, col_ref, block_ref, view_ref, recv_hbm, ytab_hbm, ztab_hbm, data_own_hbm,
                data_got_hbm, tiles_hbm, pay_hbm, got_hbm, measured_hbm, background_hbm,
                out_hbm, recv_ref, ytab_ref, ztab_ref, data_ref, mask_ref, tiles_ref, bins_ref, counts_ref,
                ratio, gathered, acc, sens, images, kyrows, out_ref, sems, out_sems):
    copies = []

    def fetch(source, target):
        copies.append(pltpu.make_async_copy(source, target, sems.at[len(copies)]))
        copies[-1].start()
        return copies[-1]

    received = [fetch(recv_hbm.at[pl.ds(8 * n, 8)], recv_ref.at[pl.ds(8 * n, 8)]) for n in range(4)]
    small = [
        fetch(pay_hbm, bins_ref.at[0]), fetch(got_hbm, bins_ref.at[1]),
        fetch(measured_hbm, counts_ref.at[0]), fetch(background_hbm, counts_ref.at[1]),
    ]
    tables = [
        fetch(ytab_hbm.at[pl.ds(256 * n, 256)], ytab_ref.at[pl.ds(256 * n, 256)]) for n in range(4)
    ]
    others = [
        fetch(ztab_hbm, ztab_ref),
        fetch(data_own_hbm.at[pl.ds(0, 2)], data_ref.at[core_ref[0]]),
        fetch(data_got_hbm, data_ref.at[1 - core_ref[0]]),
        fetch(data_own_hbm.at[2], mask_ref),
    ]
    tiles = [fetch(tiles_hbm.at[pl.ds(4 * n, 4)], tiles_ref.at[pl.ds(4 * n, 4)]) for n in range(4)]
    for copy in received:
        copy.wait()

    def block(c, b):
        return recv_ref[16 * c : 16 * (c + 1), 16 * b : 16 * (b + 1), :].astype(f32)

    lane = lax.broadcasted_iota(jnp.int32, (NZ, 128), 1)

    def image_part(c):
        tail = recv_ref[16 * c : 16 * (c + 1), 128:, :].astype(f32)
        parts = [tail[:, ZS * b : ZS * (b + 1)].reshape(NZ, 128) for b in range(3)]
        real, imag = block(c, 3), block(c, 7)
        first = pltpu.roll(real[:, :ZS].reshape(NZ, 128), 32, 1)
        second = pltpu.roll(real[:, ZS:].reshape(NZ, 128), 64, 1)
        third = pltpu.roll(imag[:, :ZS].reshape(NZ, 128), 96, 1)
        last = jnp.where(lane < 32, first, jnp.where(lane < 64, second, third))
        return jnp.concatenate(parts + [jnp.where(lane < 96, last, 0.0)], -1)

    mr_re, mr_im = image_part(0), image_part(1)
    for c in range(2):
        for b in range(4):
            real, imag = block(c, b), block(c, 4 + b)
            lanes = slice(128 * b, 128 * (b + 1))
            lanes_im = slice(HALF + 128 * b, HALF + 128 * (b + 1))
            for k in range(2):
                rows = pl.ds((2 * c + k) * NZ, NZ)
                s_re = real[:, k * ZS : (k + 1) * ZS].reshape(NZ, 128)
                s_im = imag[:, k * ZS : (k + 1) * ZS].reshape(NZ, 128)
                sens[rows, lanes] = s_re
                sens[rows, lanes_im] = s_im
                images[rows, lanes] = (s_re * mr_re[:, lanes] - s_im * mr_im[:, lanes]).astype(bf16)
                images[rows, lanes_im] = (s_re * mr_im[:, lanes] + s_im * mr_re[:, lanes]).astype(bf16)
    for copy in small:
        copy.wait()
    ratio_now = ratio_rows(
        block_ref, view_ref, bins_ref.at[0], bins_ref.at[1], counts_ref.at[0], counts_ref.at[1], ratio, gathered
    )
    for copy in tables:
        copy.wait()
    kyrows[...] = jnp.dot(images[...], ytab_ref[...], preferred_element_type=f32).astype(bf16)
    for copy in others:
        copy.wait()
    mask = mask_ref[:NZ, :].astype(f32)
    for q in range(4):
        rows = pl.ds(q * NZ, NZ)
        volume = jnp.concatenate([kyrows[rows, :HALF], kyrows[rows, HALF:]], 0)
        kspace = jnp.dot(ztab_ref[0], volume, preferred_element_type=f32)
        data = data_ref[q // 2, q % 2].astype(f32)
        misfit = jnp.concatenate(
            [mask * (kspace[:NZ] - data[:NZ]), mask * (data[NZ:] - kspace[NZ:])], 0
        ).astype(bf16)
        back = jnp.dot(ztab_ref[1], misfit, preferred_element_type=f32).astype(bf16)
        images[rows, :HALF] = back[:NZ]
        images[rows, HALF:] = back[NZ:]
    for copy in tiles:
        copy.wait()
    backproject(col_ref, ratio_now, tiles_ref, acc, out_ref)
    out_copies = []
    for n in (1, 0):
        part = (slice(None), pl.ds(2 * ZS * n, 2 * ZS))
        out_copies.append(pltpu.make_async_copy(out_ref.at[part], out_hbm.at[part], out_sems.at[n]))
    out_copies[0].start()
    for b in range(4):
        lanes = slice(128 * b, 128 * (b + 1))
        lanes_im = slice(HALF + 128 * b, HALF + 128 * (b + 1))
        table = jnp.concatenate([ytab_ref[:, lanes], ytab_ref[:, lanes_im]], 1)
        image = jnp.dot(images[...], table, preferred_element_type=f32)
        total_re = jnp.zeros((NZ, 128), f32)
        total_im = jnp.zeros((NZ, 128), f32)
        for q in range(4):
            rows = slice(q * NZ, (q + 1) * NZ)
            s_re, s_im = sens[rows, lanes], sens[rows, lanes_im]
            i_re, i_im = image[rows, :128], image[rows, 128:]
            total_re = total_re + (s_re * i_re - s_im * i_im)
            total_im = total_im - (s_re * i_im + s_im * i_re)
        for total, place in ((total_re, lanes), (total_im, lanes_im)):
            slabs = total.reshape(16, ZS, 128)
            for p in range(8):
                both = jnp.concatenate([slabs[arrived(2 * p)], slabs[arrived(2 * p + 1)]], 0)
                out_ref[p, : 2 * ZS, place] = both.astype(bf16)
    out_copies[1].start()
    for copy in out_copies:
        copy.wait()


def sum_kernel(half_ref, recv_ref, mr_own, mr_other, pet_own, pet_other):
    upper = half_ref[0] == 1
    pet = jnp.zeros((2 * ZS, ROW), f32)
    for c in range(2):
        mr = jnp.zeros((2 * ZS, ROW), f32)
        for x in range(4):
            block = recv_ref[2 * x + c].astype(f32)
            mr = mr + block[: 2 * ZS]
            pet = pet + block[2 * ZS :]
        rows = pl.ds(c * ZS, ZS)
        mr_own[rows, :] = jnp.where(upper, mr[ZS:], mr[:ZS]).astype(bf16)
        mr_other[rows, :] = jnp.where(upper, mr[:ZS], mr[ZS:]).astype(bf16)
    pet_own[...] = jnp.where(upper, pet[ZS:], pet[:ZS])
    pet_other[...] = jnp.where(upper, pet[:ZS], pet[ZS:]).astype(bf16)


def final_kernel(mr_a, mr_b, pet_a, pet_b, couple_pet_ref, couple_mr_ref, pet_out, mr_out):
    for k in range(2):
        rows = pl.ds(k * ZS, ZS)
        lanes = pl.ds(k * HALF, HALF)
        pet = pet_a[:, lanes] + pet_b[:, lanes].astype(f32) + couple_pet_ref[k]
        mr = mr_a[rows, :].astype(f32) + mr_b[rows, :].astype(f32) + couple_mr_ref[k]
        pet_out[:, k, :] = pet[:, :NY]
        mr_out[:, k, :NY] = mr[:, :NY]
        mr_out[:, k, NY:] = mr[:, HALF : HALF + NY]


def sds(shape, dtype):
    return jax.ShapeDtypeStruct(shape, dtype)


def on_device(
    pet_image, mr_image, coil_sens, kspace_data, kspace_mask, system_tiles,
    tile_subset_block, tile_col, measured, background, subset_view_blocks,
):
    core = lax.axis_index("c")
    grp = lax.axis_index(GRP)
    gz = lax.axis_index(GZ)
    core_arr = core.astype(jnp.int32).reshape(1)
    pet_rows = pet_image.reshape(ZS * NX, NY)
    mr_rows = mr_image.reshape(ZS * NX, 2 * NY)
    tiles = system_tiles.swapaxes(1, 2)

    sent = call(
        pack_kernel, sds((32, CHUNK, 128), bf16), [SMEM] + [ANY] * 2,
        [pltpu.VMEM((2 * ZS * NX, 2 * NY), bf16), pltpu.VMEM((ZS * NX, 2 * NY), f32),
         pltpu.VMEM((512, 512), bf16), pltpu.VMEM((256, 256), bf16), pltpu.VMEM((512, ROW), bf16),
         pltpu.VMEM((256, 384), bf16), pltpu.VMEM((32, CHUNK, 128), bf16),
         pltpu.SemaphoreType.DMA((8,)), pltpu.SemaphoreType.DMA((5,))],
        10**9, 4 * 10**6, "pack", ANY, 60,
    )(core_arr, coil_sens.reshape(2 * ZS * NX, 2 * NY), mr_rows)
    sent, tile_col = lax.optimization_barrier((sent, tile_col))
    recv = lax.all_to_all(sent, ("c", "y", "zl"), split_axis=0, concat_axis=0, tiled=True)

    xs = jnp.clip(2 * grp - 1 + jnp.arange(4, dtype=jnp.int32), 0, NX - 1)
    bits = [(gz >> t) & 1 for t in range(4)]
    ones = [gz & 1, (gz & 3) == 3, (gz & 7) == 7]
    zeros = [(gz & 1) == 0, (gz & 3) == 0, (gz & 7) == 0]
    after = sum(jnp.asarray(v).astype(jnp.int32) for v in ones)
    before = sum(jnp.asarray(v).astype(jnp.int32) for v in zeros)
    info = jnp.stack([gz * ZS, 2 * grp] + bits + [before, after]).astype(jnp.int32)
    pay, win, low, high = call(
        project_kernel,
        (sds((64, 128), f32), sds((12, ZS, HALF), f32), sds((48, 128), f32), sds((48, 128), f32)),
        [SMEM] * 4 + [VMEM] * 3, [pltpu.VMEM((16, NY), f32)],
        10**7, 4 * 10**6, "project", VMEM, 8,
    )(info, tile_col, tile_subset_block, xs, pet_rows, mr_rows, tiles)
    got = []
    for step in range(4):
        got.append(lax.ppermute(pay, GZ, [(i, i ^ (2 ** (step + 1) - 1)) for i in range(16)]))
        if step == 0:
            kspace_data, got[0] = lax.optimization_barrier((kspace_data, got[0]))
        if step < 3:
            edge = jnp.where(bits[step + 1] == 1, low, high)
            pay = jnp.concatenate([pay[:16] + got[step][:16], edge], 0)
    data_own, data_out = call(
        prepare_kernel, (sds((3, 2 * NZ, HALF), bf16), sds((2, 2 * NZ, HALF), bf16)),
        [SMEM, VMEM, VMEM], [], 10**6, 3 * 10**6, "prepare", VMEM, 8,
    )(core_arr, kspace_data.transpose(0, 2, 3, 1), kspace_mask.T)
    data_got = lax.ppermute(data_out, "c", [(0, 1), (1, 0)])
    couple_pet, couple_mr = call(
        coupling_kernel, (sds((2, ZS, HALF), f32), sds((2, ZS, ROW), f32)),
        [SMEM] + [VMEM] * 5,
        [pltpu.VMEM((12, 24, HALF), f32), pltpu.VMEM((4, 24, HALF), f32),
         pltpu.VMEM((3, 16, HALF), f32)],
        10**6, 10**6, "coupling", VMEM, 8,
    )(info, win, *got)

    parts = call(
        coil_kernel, sds((8, 4 * ZS, ROW), bf16), [SMEM] * 4 + [ANY] * 10,
        [pltpu.VMEM((32, CHUNK, 128), bf16), pltpu.VMEM((ROW, ROW), bf16),
         pltpu.VMEM((2, 2 * NZ, 2 * NZ), bf16), pltpu.VMEM((2, 2, 2 * NZ, HALF), bf16),
         pltpu.VMEM((2 * NZ, HALF), bf16), pltpu.VMEM((16, NY, 128), bf16),
         pltpu.VMEM((2, 64, 128), f32), pltpu.VMEM((2, 64, 128), f32),
         pltpu.VMEM((16, 128), f32), pltpu.VMEM((16, 128), f32), pltpu.VMEM((4, ZS * NX, 128), f32),
         pltpu.VMEM((4 * NZ, ROW), f32), pltpu.VMEM((4 * NZ, ROW), bf16),
         pltpu.VMEM((4 * NZ, ROW), bf16), pltpu.VMEM((8, 4 * ZS, ROW), bf16),
         pltpu.SemaphoreType.DMA((20,)), pltpu.SemaphoreType.DMA((2,))],
        5 * 10**9, 6 * 10**6, "coils", ANY, 61,
    )(core_arr, tile_col, tile_subset_block, subset_view_blocks, recv, y_table(), z_tables(), data_own,
      data_got, tiles, pay, got[3], measured, background)

    both = lax.all_to_all(parts, ("x", "c"), split_axis=0, concat_axis=0, tiled=True)
    half = lax.axis_index("zh").astype(jnp.int32).reshape(1)
    mr_own, mr_other, pet_own, pet_other = call(
        sum_kernel,
        (sds((2 * ZS, ROW), bf16), sds((2 * ZS, ROW), bf16), sds((ZS, ROW), f32), sds((ZS, ROW), bf16)),
        [SMEM, VMEM], [], 10**6, 10**6, "sums",
    )(half, both)
    places = [(zh, p, j) for zh in range(2) for p in range(8) for j in range(16)]
    mr_a = lax.ppermute(
        mr_own, GRP + GZ, [((zh * 8 + p) * 16 + j, j * 16 + 2 * p + 1 * zh) for zh, p, j in places]
    )
    mr_b = lax.ppermute(
        mr_other, GRP + GZ, [((zh * 8 + p) * 16 + j, j * 16 + 2 * p + 1 * (1 - zh)) for zh, p, j in places]
    )
    pet_got = lax.ppermute(pet_other, "zh", [(0, 1), (1, 0)])
    return call(
        final_kernel, (sds((ZS, 2, NY), f32), sds((ZS, 2, 2 * NY), f32)), [VMEM] * 6, [],
        10**5, 10**6, "final",
    )(mr_a, mr_b, pet_own, pet_got, couple_pet, couple_mr)


def solution(mesh):
    fine = Mesh(mesh.devices.reshape(2, 4, 2, 4, 4), ("zh", "x", "c", "zl", "y"))
    placed = (
        P(GZ, None, None),
        P(GZ, None, None),
        P(GRP, GZ, None, None),
        P(GRP, None, GZ, None),
        P(),
        P(GRP + GZ, None, None),
        P(GRP + GZ),
        P(GRP + GZ),
        P(GRP, None),
        P(GRP, None),
        P(GRP),
    )
    return jax.shard_map(
        on_device,
        mesh=fine,
        in_specs=placed,
        out_specs=(P(GZ, GRP, None), P(GZ, GRP, None)),
        check_vma=False,
    )
```
